128 devices in a mesh: tm: 16 (over x_lo, y, core), patch: 8 (over z, x_hi).
Axes of the slice: x: 4 (x_hi: 2, x_lo: 2; x = x_hi * 2 + x_lo), y: 4, z: 4, core: 2. Of those that a mesh axis runs over, the one named last changes fastest.
Arguments:
- frames_in: bfloat16 [128, 512, 1024], P('tm', 'patch'), may hold values from -6 to 6
- codes: int32 [128, 512], P('tm', 'patch'), may hold values from 0 to 1023
- gain_space: float32 [1024], replicated, may hold values from 0.1 to 1.9
- qkv_space: bfloat16 [1024, 3072], replicated, may hold values from -0.1875 to 0.1875
- out_space: bfloat16 [1024, 1024], replicated, may hold values from -0.75 to 0.75
- scale_space: float32 [16], replicated, may hold values from 3 to 12
- gain_time: float32 [1024], replicated, may hold values from 0.1 to 1.9
- qkv_time: bfloat16 [1024, 3072], replicated, may hold values from -0.1875 to 0.1875
- out_time: bfloat16 [1024, 1024], replicated, may hold values from -0.75 to 0.75
- scale_time: float32 [16], replicated, may hold values from 3 to 12
- codebook: bfloat16 [1024, 1024], replicated, may hold values from -6 to 6
Outputs:
- encoded: bfloat16 [128, 512, 1024], P('tm', 'patch')
- commitment: bfloat16 [128, 512, 1024], P('tm', 'patch')
The draws below stay inside these ranges and needn't reach their ends.
All inputs are finite; a program needn't handle non-finite values.
Results may differ from the reference program's by a relative error of at most 0.02.
Values may be sent and summed in bfloat16 or wider, within the bound.
No kernel may reach another device: no remote copies, remote signals or barrier semaphores. Data moves between devices by JAX's collectives and lax.ppermute only.
A program may use at most 192 MiB of HBM per device.

```python
import math
import jax
import jax.numpy as jnp
from jax import lax

D = 1024
H = 16
HD = 64
CODES = 1024
F = 128
P_SIZE = 512


def plant(values, own_key, low, largest):
    extent = values.shape
    index_at = [jax.random.randint(jax.random.fold_in(own_key, axis), (), 0, extent[axis]) for axis in range(len(extent))]
    values = values.at[tuple(index_at)].set(low)
    longest = extent.index(max(extent))
    index_at[longest] = (index_at[longest] + 1) % extent[longest]
    return values.at[tuple(index_at)].set(largest)


def block_levels(own_key, shape, split, smallest, top_value):
    def one(position, shards_of):
        steps = jax.random.uniform(jax.random.fold_in(jax.random.fold_in(own_key, 6), position), (shards_of,), jnp.float32, smallest / len(split), top_value / len(split))
        return jnp.repeat(jnp.exp(steps), shape[position] // shards_of).reshape((-1,) + (1,) * (len(shape) - position - 1))

    level = one(*split[0])
    for cut in split[1:]:
        level = level * one(*cut)
    return level


def centred(key, dims, width, reach, pieces=(), kind=jnp.bfloat16):
    array = jax.random.normal(key, dims, jnp.float32) * width
    if len(pieces) > 0:
        array = block_levels(key, dims, pieces, -0.22, 0.18) * array
    return jnp.clip(array, min=-reach, max=reach).astype(kind)


def setup_inputs(seed: int = 0) -> dict:
    key_of = jax.random.split(jax.random.key(seed), 12)
    frames_in = centred(key_of[0], (F, P_SIZE, D), 1.0, 6.0, ((0, 16), (1, 8)))
    codes = plant(jax.random.randint(key_of[1], (F, P_SIZE), 0, CODES), jax.random.fold_in(key_of[1], 1), 0, CODES - 1).astype(jnp.int32)
    gain_space = jnp.clip(1.0 + 0.18 * jax.random.normal(key_of[2], (D,), jnp.float32), 0.1, 1.9)
    qkv_space = centred(key_of[3], (D, 3 * D), D ** -0.5, 0.1875)
    out_space = centred(key_of[4], (D, D), (D // 16) ** -0.5, 0.75)
    scale_space = jnp.clip(jnp.exp(jax.random.uniform(key_of[5], (H,), jnp.float32, math.log(3.0), math.log(12.0))), 3.0, 12.0)
    gain_time = jnp.clip(1.0 + 0.18 * jax.random.normal(key_of[6], (D,), jnp.float32), 0.1, 1.9)
    qkv_time = centred(key_of[7], (D, 3 * D), D ** -0.5, 0.1875)
    out_time = centred(key_of[8], (D, D), (D // 16) ** -0.5, 0.75)
    scale_time = jnp.clip(jnp.exp(jax.random.uniform(key_of[9], (H,), jnp.float32, math.log(3.0), math.log(12.0))), 3.0, 12.0)
    codebook = centred(key_of[10], (CODES, D), 1.0, 6.0)
    return dict(frames_in=frames_in, codes=codes, gain_space=gain_space, qkv_space=qkv_space, out_space=out_space, scale_space=scale_space, gain_time=gain_time, qkv_time=qkv_time, out_time=out_time, scale_time=scale_time, codebook=codebook)


def norm_rows(stream, gain):
    wide = stream.astype(jnp.float32)
    return (wide * lax.rsqrt(lax.optimization_barrier(jnp.mean(wide * wide, -1, keepdims=True)) + 1e-05) * gain).astype(jnp.bfloat16)

def project(stream, gain, weights, scale):
    normed = norm_rows(stream, gain)
    lead = normed.shape[:-1]
    qkv = jnp.dot(normed.reshape(-1, D), weights, preferred_element_type=jnp.float32)
    query = qkv[:, :D].reshape(-1, H, HD)
    key = qkv[:, D:2 * D].reshape(-1, H, HD)
    value = qkv[:, 2 * D:]
    query = query * lax.rsqrt(lax.optimization_barrier(jnp.mean(query * query, -1, keepdims=True)) + 1e-06) * (scale[:, None] / HD)
    key = key * lax.rsqrt(lax.optimization_barrier(jnp.mean(key * key, -1, keepdims=True)) + 1e-06)
    return (query.reshape(lead + (D,)).astype(jnp.bfloat16), key.reshape(lead + (D,)).astype(jnp.bfloat16), value.reshape(lead + (D,)).astype(jnp.bfloat16))

def frame_attend(items):
    query, key, value = items
    count = query.shape[0]
    query = query.reshape(count, H, HD).astype(jnp.float32)
    key = key.reshape(count, H, HD).astype(jnp.float32)
    value = value.reshape(count, H, HD).astype(jnp.float32)
    scores = jnp.einsum('phd,qhd->hpq', query, key)
    weight = jnp.exp(scores).astype(jnp.bfloat16).astype(jnp.float32)
    total = jnp.einsum('hpq,qhd->phd', weight, value)
    denom = lax.optimization_barrier(jnp.sum(weight, -1)).T
    return (total / denom[:, :, None]).reshape(count, D).astype(jnp.bfloat16)

def reference(frames_in, codes, gain_space, qkv_space, out_space, scale_space, gain_time, qkv_time, out_time, scale_time, codebook):
    query, key, value = project(frames_in, gain_space, qkv_space, scale_space)
    attn_s = lax.map(frame_attend, (query, key, value))
    stream = frames_in.astype(jnp.float32) + jnp.dot(attn_s.reshape(-1, D), out_space, preferred_element_type=jnp.float32).reshape(F, P_SIZE, D)
    query, key, value = project(stream, gain_time, qkv_time, scale_time)
    query = query.reshape(F, P_SIZE, H, HD).astype(jnp.float32)
    key = key.reshape(F, P_SIZE, H, HD).astype(jnp.float32)
    value = value.reshape(F, P_SIZE, H, HD).astype(jnp.float32)
    scores = jnp.einsum('fphd,gphd->phfg', query, key)
    frame_ids = jnp.arange(F, dtype=jnp.int32)
    causal = frame_ids[:, None] >= frame_ids[None, :]
    weight = jnp.where(causal, jnp.exp(scores), 0.0).astype(jnp.bfloat16).astype(jnp.float32)
    total = jnp.einsum('phfg,gphd->fphd', weight, value)
    denom = jnp.transpose(lax.optimization_barrier(jnp.sum(weight, -1)), (2, 0, 1))
    attn_t = (total / denom[..., None]).reshape(F * P_SIZE, D).astype(jnp.bfloat16)
    output = stream + jnp.dot(attn_t, out_time, preferred_element_type=jnp.float32).reshape(F, P_SIZE, D)
    chosen = jnp.take(codebook, codes, axis=0).astype(jnp.float32)
    return (output.astype(jnp.bfloat16), (output - chosen).astype(jnp.bfloat16))
```

```python
import functools
import math

import jax
import jax.numpy as jnp
from jax import lax
from jax.experimental import pallas as pl
from jax.experimental.pallas import tpu as pltpu
from jax.sharding import PartitionSpec as P

H = 16
HD = 64
D = 1024
GROUP = 256
PAIR = 128
LOG2E = math.log2(math.e)
VMEM_LIMIT = 48 * 1024 * 1024
f32 = jnp.float32
bf16 = jnp.bfloat16


def iota(shape, axis):
    return lax.broadcasted_iota(jnp.int32, shape, axis)


def same_head_mean():
    same = (iota((GROUP, GROUP), 0) // HD) == (iota((GROUP, GROUP), 1) // HD)
    return jnp.where(same, f32(1.0 / HD), f32(0.0)).astype(bf16)


def norm_rows(wide, gain):
    mean = jnp.mean(wide * wide, -1, keepdims=True)
    return (wide * lax.rsqrt(mean + 1e-5) * gain).astype(bf16)


def head_norm(block, averager):
    square = (block * block).astype(bf16)
    mean = jnp.dot(square, averager, preferred_element_type=f32)
    return block * lax.rsqrt(mean + 1e-6)


def scale_row(scale_ref, first_head):
    head = iota((1, GROUP), 1) // HD
    row = jnp.full((1, GROUP), scale_ref[first_head], f32)
    for h in range(1, GROUP // HD):
        row = jnp.where(head == h, scale_ref[first_head + h], row)
    return row * f32(LOG2E / HD)


def key_pair(key):
    low = iota(key.shape, 1) < HD
    zero = jnp.zeros_like(key)
    return jnp.concatenate([jnp.where(low, key, zero), jnp.where(low, zero, key)], 0)


def value_pair(value):
    low = iota(value.shape, 1) < HD
    zero = jnp.zeros_like(value)
    one = jnp.ones_like(value)
    first = jnp.concatenate([jnp.where(low, value, zero), jnp.where(low, one, zero)], 1)
    second = jnp.concatenate([jnp.where(low, zero, value), jnp.where(low, zero, one)], 1)
    return jnp.concatenate([first, second], 0)


def weight_copies(qkv_hbm, qkv_buf, sems):
    copies = []
    for part in range(3):
        for g in range(D // GROUP):
            copies.append(
                pltpu.make_async_copy(
                    qkv_hbm.at[:, pl.ds(part * D + g * GROUP, GROUP)],
                    qkv_buf.at[:, pl.ds(part * D + g * GROUP, GROUP)],
                    sems.at[part, g],
                )
            )
    return copies


def spatial_kernel(x_ref, gain_ref, scale_ref, qkv_hbm, out_hbm, o_ref, qkv_buf, out_buf, normed, attn, sems, out_sem):
    copies = weight_copies(qkv_hbm, qkv_buf, sems)
    for g in range(4):
        for part in range(3):
            copies[part * 4 + g].start()
    out_copy = pltpu.make_async_copy(out_hbm, out_buf, out_sem)
    out_copy.start()
    normed[...] = norm_rows(x_ref[...].astype(f32), gain_ref[...])
    averager = same_head_mean()
    for g in range(4):
        for part in range(3):
            copies[part * 4 + g].wait()
        src = normed[...]
        col = g * GROUP
        q = jnp.dot(src, qkv_buf[:, col : col + GROUP], preferred_element_type=f32)
        k = jnp.dot(src, qkv_buf[:, D + col : D + col + GROUP], preferred_element_type=f32)
        v = jnp.dot(src, qkv_buf[:, 2 * D + col : 2 * D + col + GROUP], preferred_element_type=f32)
        q = (head_norm(q, averager) * scale_row(scale_ref, 4 * g)).astype(bf16)
        k = head_norm(k, averager).astype(bf16)
        v = v.astype(bf16)
        for pair in range(2):
            lanes = slice(pair * PAIR, (pair + 1) * PAIR)
            keys = key_pair(k[:, lanes])
            values = value_pair(v[:, lanes])
            for r in range(2):
                rows = slice(r * 256, (r + 1) * 256)
                s = lax.dot_general(q[rows, lanes], keys, (((1,), (1,)), ((), ())), preferred_element_type=f32)
                w = jnp.exp2(s).astype(bf16)
                o = jnp.dot(w, values, preferred_element_type=f32)
                attn[rows, col + pair * PAIR : col + (pair + 1) * PAIR] = (o[:, :PAIR] / o[:, PAIR:]).astype(bf16)
    out_copy.wait()
    half = D // 2
    low = iota((1, 8, half), 1) < 4
    stream = x_ref[...].astype(f32) + jnp.dot(attn[...], out_buf[...], preferred_element_type=f32)
    a = stream[:, :half].reshape(64, 8, half)
    b = stream[:, half:].reshape(64, 8, half)
    even = jnp.where(low, a, pltpu.roll(b, 4, 1)).astype(bf16)
    odd = jnp.where(low, pltpu.roll(a, 4, 1), b).astype(bf16)
    for j in range(8):
        o_ref[:, j] = jnp.stack([even[8 * j : 8 * j + 8], odd[8 * j : 8 * j + 8]], 1).reshape(16, 8, half)


def temporal_kernel(x_ref, gain_ref, scale_ref, qkv_hbm, out_hbm, o_ref, qkv_buf, out_buf, stream, normed, attn, sems, out_sem):
    copies = weight_copies(qkv_hbm, qkv_buf, sems)
    for g in range(4):
        for part in range(3):
            copies[part * 4 + g].start()
    out_copy = pltpu.make_async_copy(out_hbm, out_buf, out_sem)
    out_copy.start()
    half = D // 2
    want = iota((512, 1024), 0)
    have = iota((512, 1024), 1)
    source = (want & 127) * 8 + (want >> 7)
    recv = x_ref[...].reshape(1024, half)
    one = f32(1.0)
    nil = f32(0.0)
    stream[:, :half] = jnp.dot(jnp.where(have == source, one, nil).astype(bf16), recv, preferred_element_type=f32)
    stream[:, half:] = jnp.dot(jnp.where(have == source + 4, one, nil).astype(bf16), recv, preferred_element_type=f32)
    normed[...] = norm_rows(stream[...], gain_ref[...])
    averager = same_head_mean()
    causal = iota((128, 256), 0) >= (iota((128, 256), 1) & 127)
    for g in range(4):
        for part in range(3):
            copies[part * 4 + g].wait()
        src = normed[...]
        col = g * GROUP
        q = jnp.dot(src, qkv_buf[:, col : col + GROUP], preferred_element_type=f32)
        k = jnp.dot(src, qkv_buf[:, D + col : D + col + GROUP], preferred_element_type=f32)
        v = jnp.dot(src, qkv_buf[:, 2 * D + col : 2 * D + col + GROUP], preferred_element_type=f32)
        q = (head_norm(q, averager) * scale_row(scale_ref, 4 * g)).astype(bf16)
        k = head_norm(k, averager).astype(bf16)
        v = v.astype(bf16)
        for pair in range(2):
            lanes = slice(pair * PAIR, (pair + 1) * PAIR)
            for p in range(4):
                rows = slice(p * 128, (p + 1) * 128)
                keys = key_pair(k[rows, lanes])
                values = value_pair(v[rows, lanes])
                s = lax.dot_general(q[rows, lanes], keys, (((1,), (1,)), ((), ())), preferred_element_type=f32)
                w = jnp.where(causal, jnp.exp2(s), nil).astype(bf16)
                o = jnp.dot(w, values, preferred_element_type=f32)
                attn[rows, col + pair * PAIR : col + (pair + 1) * PAIR] = (o[:, :PAIR] / o[:, PAIR:]).astype(bf16)
    out_copy.wait()
    output = (stream[...] + jnp.dot(attn[...], out_buf[...], preferred_element_type=f32)).astype(bf16)
    want = iota((512, 512), 0)
    source = (want & 3) * 128 + (want >> 2)
    move = jnp.where(iota((512, 512), 1) == source, one, nil).astype(bf16)
    o_ref[...] = jnp.dot(move, output, preferred_element_type=f32).astype(bf16)


def chosen_kernel(codes_ref, codebook_ref, o_ref):
    hot = jnp.where(codes_ref[...] == iota((512, D), 1), f32(1.0), f32(0.0)).astype(bf16)
    o_ref[...] = jnp.dot(hot, codebook_ref[...], preferred_element_type=f32).astype(bf16)


def final_kernel(x_ref, chosen_ref, enc_ref, com_ref):
    want = iota((512, 512), 0)
    source = ((want >> 2) & 15) * 32 + (want >> 6) * 4 + (want & 3)
    move = jnp.where(iota((512, 512), 1) == source, f32(1.0), f32(0.0)).astype(bf16)
    output = jnp.dot(move, x_ref[...], preferred_element_type=f32)
    enc_ref[...] = output.astype(bf16)
    com_ref[...] = (output - chosen_ref[...].astype(f32)).astype(bf16)


VM = pl.BlockSpec(memory_space=pltpu.VMEM)
SM = pl.BlockSpec(memory_space=pltpu.SMEM)
ANY = pl.BlockSpec(memory_space=pl.ANY)
PARAMS = pltpu.CompilerParams(vmem_limit_bytes=VMEM_LIMIT)


def cost(gmac, mbytes):
    return pl.CostEstimate(flops=int(2e9 * gmac), bytes_accessed=int(1e6 * mbytes), transcendentals=0)


def weight_scratch():
    return [pltpu.VMEM((D, 3 * D), bf16), pltpu.VMEM((D, D), bf16)]


def shards(frames_in, codes, gain_space, qkv_space, out_space, scale_space, gain_time, qkv_time, out_time, scale_time, codebook):
    x = lax.all_to_all(frames_in, "patch", 0, 0, tiled=True).reshape(512, D)
    chosen = pl.pallas_call(
        chosen_kernel,
        out_shape=jax.ShapeDtypeStruct((512, D), bf16),
        in_specs=[VM, VM],
        out_specs=VM,
        compiler_params=PARAMS,
        cost_estimate=cost(0.6, 6),
        name="chosen",
    )(codes.reshape(512, 1), codebook)
    sems = [pltpu.SemaphoreType.DMA((3, 4)), pltpu.SemaphoreType.DMA]
    stream = pl.pallas_call(
        spatial_kernel,
        out_shape=jax.ShapeDtypeStruct((16, 8, 8, 512), bf16),
        in_specs=[VM, VM, SM, ANY, ANY],
        out_specs=VM,
        scratch_shapes=weight_scratch() + [pltpu.VMEM((512, D), bf16)] * 2 + sems,
        compiler_params=PARAMS,
        cost_estimate=cost(5, 10),
        name="spatial",
    )(x, gain_space.reshape(1, D), scale_space, qkv_space, out_space)
    stream = lax.all_to_all(stream.reshape(128, 8, 512), ("tm", "patch"), 0, 0, tiled=True)
    output = pl.pallas_call(
        temporal_kernel,
        out_shape=jax.ShapeDtypeStruct((512, D), bf16),
        in_specs=[VM, VM, SM, ANY, ANY],
        out_specs=VM,
        scratch_shapes=weight_scratch() + [pltpu.VMEM((512, D), f32)] + [pltpu.VMEM((512, D), bf16)] * 2 + sems,
        compiler_params=PARAMS,
        cost_estimate=cost(4, 10),
        name="temporal",
    )(stream, gain_time.reshape(1, D), scale_time, qkv_time, out_time)
    output = lax.all_to_all(output.reshape(16, 32, D), "tm", 0, 0, tiled=True).reshape(512, D)
    encoded, commitment = pl.pallas_call(
        final_kernel,
        out_shape=[jax.ShapeDtypeStruct((512, D), bf16)] * 2,
        in_specs=[VM, VM],
        out_specs=[VM, VM],
        compiler_params=PARAMS,
        cost_estimate=cost(0.3, 4),
        name="final",
    )(output, chosen)
    return encoded.reshape(8, 64, D), commitment.reshape(8, 64, D)


def solution(mesh):
    rows = P("tm", "patch", None)
    return jax.shard_map(
        shards,
        mesh=mesh,
        in_specs=(rows, P("tm", "patch")) + (P(),) * 9,
        out_specs=(rows, rows),
        check_vma=False,
    )
```

```python
import functools
import math

import jax
import jax.numpy as jnp
from jax import lax
from jax.experimental import pallas as pl
from jax.experimental.pallas import tpu as pltpu
from jax.sharding import PartitionSpec as P

H = 16
HD = 64
D = 1024
GROUP = 256
PAIR = 128
ROWS = 256
LOG2E = math.log2(math.e)
f32 = jnp.float32
bf16 = jnp.bfloat16


def iota(shape, axis):
    return lax.broadcasted_iota(jnp.int32, shape, axis)


def same_head_mean():
    same = (iota((GROUP, GROUP), 0) // HD) == (iota((GROUP, GROUP), 1) // HD)
    return jnp.where(same, f32(1.0 / HD), f32(0.0)).astype(bf16)


def norm_rows(wide, gain):
    mean = jnp.mean(wide * wide, -1, keepdims=True)
    return (wide * lax.rsqrt(mean + 1e-5) * gain).astype(bf16)


def head_norm(block, averager):
    square = (block * block).astype(bf16)
    mean = jnp.dot(square, averager, preferred_element_type=f32)
    return block * lax.rsqrt(mean + 1e-6)


def scale_row(scale_ref, first_head):
    head = iota((1, GROUP), 1) // HD
    row = jnp.full((1, GROUP), scale_ref[first_head], f32)
    for h in range(1, GROUP // HD):
        row = jnp.where(head == h, scale_ref[first_head + h], row)
    return row * f32(LOG2E / HD)


def key_pair(key):
    low = iota(key.shape, 1) < HD
    zero = jnp.zeros_like(key)
    return jnp.concatenate([jnp.where(low, key, zero), jnp.where(low, zero, key)], 0)


def value_pair(value):
    low = iota(value.shape, 1) < HD
    zero = jnp.zeros_like(value)
    one = jnp.ones_like(value)
    first = jnp.concatenate([jnp.where(low, value, zero), jnp.where(low, one, zero)], 1)
    second = jnp.concatenate([jnp.where(low, zero, value), jnp.where(low, zero, one)], 1)
    return jnp.concatenate([first, second], 0)


def weight_copies(qkv_hbm, qkv_buf, sems):
    return [
        [
            pltpu.make_async_copy(
                qkv_hbm.at[:, pl.ds(part * D + g * GROUP, GROUP)],
                qkv_buf.at[:, pl.ds(part * D + g * GROUP, GROUP)],
                sems.at[part, g],
            )
            for part in range(3)
        ]
        for g in range(D // GROUP)
    ]


def row_copies(source, target, sems, count):
    return [
        pltpu.make_async_copy(source.at[pl.ds(n * count, count)], target.at[pl.ds(n * count, count)], sems.at[n])
        for n in range(source.shape[0] // count)
    ]


def project(normed, qkv, scale_ref, averager, g):
    q, k, v = (
        jnp.dot(normed, qkv[:, part * D + g * GROUP : part * D + (g + 1) * GROUP], preferred_element_type=f32)
        for part in range(3)
    )
    q = (head_norm(q, averager) * scale_row(scale_ref, 4 * g)).astype(bf16)
    return q, head_norm(k, averager).astype(bf16), v.astype(bf16)


def weighted_mean(weights, values):
    o = jnp.dot(weights, values, preferred_element_type=f32)
    return (o[:, :PAIR] / o[:, PAIR:]).astype(bf16)


def logits(q, unit):
    lanes, rows, keys, _ = unit
    return lax.dot_general(q[rows, lanes], keys, (((1,), (1,)), ((), ())), preferred_element_type=f32)


def spatial_kernel(
    x_hbm, gain_hbm, scale_ref, qkv_hbm, out_hbm, o_hbm,
    x, gain, qkv_buf, out_buf, normed, attn, o, x_sems, gain_sem, sems, out_sem, o_sems,
):
    x_copies = row_copies(x_hbm, x, x_sems, 128)
    gain_copy = pltpu.make_async_copy(gain_hbm, gain, gain_sem)
    copies = weight_copies(qkv_hbm, qkv_buf, sems)
    out_copy = pltpu.make_async_copy(out_hbm, out_buf, out_sem)
    gain_copy.start()
    for copy in x_copies + copies[0]:
        copy.start()
    gain_copy.wait()
    for n, copy in enumerate(x_copies):
        copy.wait()
        rows = slice(128 * n, 128 * (n + 1))
        normed[rows, :] = norm_rows(x[rows, :].astype(f32), gain[...])
    averager = same_head_mean()
    for g in range(4):
        for copy in copies[g]:
            copy.wait()
        for copy in copies[g + 1] if g < 3 else [out_copy]:
            copy.start()
        q, k, v = project(normed[...], qkv_buf, scale_ref, averager, g)
        units = []
        for pair in range(2):
            lanes = slice(pair * PAIR, (pair + 1) * PAIR)
            keys = key_pair(k[:, lanes])
            values = value_pair(v[:, lanes])
            for r in range(0, 512, ROWS):
                units.append((lanes, slice(r, r + ROWS), keys, values))
        s = logits(q, units[0])
        for n, (lanes, rows, keys, values) in enumerate(units):
            later = logits(q, units[n + 1]) if n + 1 < len(units) else None
            w = jnp.exp2(s).astype(bf16)
            ratio = weighted_mean(w, values)
            attn[rows, g * GROUP + lanes.start : g * GROUP + lanes.stop] = ratio
            s = later
    out_copy.wait()
    half = D // 2
    low = iota((1, 8, half), 1) < 4
    stores = []
    for n in range(2):
        rows = slice(256 * n, 256 * (n + 1))
        stream = x[rows, :].astype(f32) + jnp.dot(attn[rows, :], out_buf[...], preferred_element_type=f32)
        a = stream[:, :half].reshape(32, 8, half)
        b = stream[:, half:].reshape(32, 8, half)
        even = jnp.where(low, a, pltpu.roll(b, 4, 1)).astype(bf16)
        odd = jnp.where(low, pltpu.roll(a, 4, 1), b).astype(bf16)
        for j in range(4):
            runs = jnp.stack([even[8 * j : 8 * j + 8], odd[8 * j : 8 * j + 8]], 1)
            o[:, 4 * n + j] = runs.reshape(16, 8, half)
        store = pltpu.make_async_copy(o.at[:, pl.ds(4 * n, 4)], o_hbm.at[:, pl.ds(4 * n, 4)], o_sems.at[n])
        store.start()
        stores.append(store)
    for store in stores:
        store.wait()


def temporal_kernel(
    x_hbm, gain_hbm, scale_ref, qkv_hbm, out_hbm, o_hbm,
    x, gain, qkv_buf, out_buf, stream, normed, attn, o, x_sems, gain_sem, sems, out_sem, o_sems,
):
    x_copies = row_copies(x_hbm, x, x_sems, 32)
    gain_copy = pltpu.make_async_copy(gain_hbm, gain, gain_sem)
    copies = weight_copies(qkv_hbm, qkv_buf, sems)
    out_copy = pltpu.make_async_copy(out_hbm, out_buf, out_sem)
    gain_copy.start()
    for copy in x_copies + copies[0]:
        copy.start()
    half = D // 2
    one = f32(1.0)
    nil = f32(0.0)
    want = iota((128, 256), 0)
    source = (want & 31) * 8 + (want >> 5)
    first = jnp.where(iota((128, 256), 1) == source, one, nil).astype(bf16)
    second = jnp.where(iota((128, 256), 1) == source + 4, one, nil).astype(bf16)
    gain_copy.wait()
    for b, copy in enumerate(x_copies):
        copy.wait()
        recv = x[32 * b : 32 * (b + 1)].reshape(256, half)
        block = jnp.concatenate(
            [
                jnp.dot(first, recv, preferred_element_type=f32),
                jnp.dot(second, recv, preferred_element_type=f32),
            ],
            1,
        )
        ready = norm_rows(block, gain[...])
        for p in range(4):
            rows = slice(p * 128 + 32 * b, p * 128 + 32 * (b + 1))
            stream[rows, :] = block[32 * p : 32 * (p + 1)]
            normed[rows, :] = ready[32 * p : 32 * (p + 1)]
    averager = same_head_mean()
    causal = (iota((256, 256), 0) & 127) >= (iota((256, 256), 1) & 127)
    for g in range(4):
        for copy in copies[g]:
            copy.wait()
        for copy in copies[g + 1] if g < 3 else [out_copy]:
            copy.start()
        q, k, v = project(normed[...], qkv_buf, scale_ref, averager, g)
        for pair in range(2):
            lanes = slice(pair * PAIR, (pair + 1) * PAIR)
            for p in range(0, 4, 2):
                one_rows = slice(p * 128, (p + 1) * 128)
                two_rows = slice((p + 1) * 128, (p + 2) * 128)
                blank = jnp.zeros((128, PAIR), bf16)
                queries = jnp.concatenate(
                    [
                        jnp.concatenate([q[one_rows, lanes], blank], 1),
                        jnp.concatenate([blank, q[two_rows, lanes]], 1),
                    ],
                    0,
                )
                keys = jnp.concatenate([key_pair(k[one_rows, lanes]), key_pair(k[two_rows, lanes])], 1)
                s = lax.dot_general(queries, keys, (((1,), (1,)), ((), ())), preferred_element_type=f32)
                w = jnp.where(causal, jnp.exp2(s), nil).astype(bf16)
                for n, rows in enumerate((one_rows, two_rows)):
                    ratio = weighted_mean(w[n * 128 : (n + 1) * 128], value_pair(v[rows, lanes]))
                    attn[rows, g * GROUP + lanes.start : g * GROUP + lanes.stop] = ratio
    out_copy.wait()
    want = iota((256, 256), 0)
    source = (want & 3) * 64 + (want >> 2)
    move = jnp.where(iota((256, 256), 1) == source, one, nil).astype(bf16)
    stores = []
    for b in range(2):
        pick = [slice(p * 128 + 64 * b, p * 128 + 64 * (b + 1)) for p in range(4)]
        mixed = jnp.concatenate([attn[rows, :] for rows in pick], 0)
        base = jnp.concatenate([stream[rows, :] for rows in pick], 0)
        output = (base + jnp.dot(mixed, out_buf[...], preferred_element_type=f32)).astype(bf16)
        rows = pl.ds(256 * b, 256)
        o[rows, :] = jnp.dot(move, output, preferred_element_type=f32).astype(bf16)
        store = pltpu.make_async_copy(o.at[rows, :], o_hbm.at[rows, :], o_sems.at[b])
        store.start()
        stores.append(store)
    for store in stores:
        store.wait()


def chosen_kernel(codes_ref, codebook_ref, o_hbm, rows, sem):
    hot = jnp.where(codes_ref[...] == iota((512, D), 1), f32(1.0), f32(0.0)).astype(bf16)
    rows[...] = jnp.dot(hot, codebook_ref[...], preferred_element_type=f32).astype(bf16)
    store = pltpu.make_async_copy(rows, o_hbm, sem)
    store.start()
    store.wait()


def final_kernel(x_ref, chosen_hbm, enc_hbm, com_hbm, chosen, enc, com, sems):
    load = pltpu.make_async_copy(chosen_hbm, chosen, sems.at[0])
    load.start()
    stores = []
    want = iota((128, 128), 0)
    source = ((want >> 2) & 15) * 8 + (want >> 6) * 4 + (want & 3)
    move = jnp.where(iota((128, 128), 1) == source, f32(1.0), f32(0.0)).astype(bf16)
    for n in range(4):
        rows = pl.ds(n * 128, 128)
        block = x_ref[:, 8 * n : 8 * (n + 1), :].reshape(128, D)
        output = jnp.dot(move, block, preferred_element_type=f32)
        enc[rows, :] = output.astype(bf16)
        store = pltpu.make_async_copy(enc.at[rows, :], enc_hbm.at[rows, :], sems.at[1 + 2 * n])
        store.start()
        stores.append(store)
        if n == 0:
            load.wait()
        com[rows, :] = (output - chosen[rows, :].astype(f32)).astype(bf16)
        store = pltpu.make_async_copy(com.at[rows, :], com_hbm.at[rows, :], sems.at[2 + 2 * n])
        store.start()
        stores.append(store)
    for store in stores:
        store.wait()


VM = pl.BlockSpec(memory_space=pltpu.VMEM)
HBM = pl.BlockSpec(memory_space=pltpu.HBM)
SM = pl.BlockSpec(memory_space=pltpu.SMEM)


def params(limit):
    return pltpu.CompilerParams(vmem_limit_bytes=limit)


def cost(gmac, mbytes):
    return pl.CostEstimate(flops=int(2e9 * gmac), bytes_accessed=int(1e6 * mbytes), transcendentals=0)


def shards(frames_in, codes, gain_space, qkv_space, out_space, scale_space, gain_time, qkv_time, out_time, scale_time, codebook):
    x = lax.all_to_all(frames_in, "patch", 0, 0, tiled=True).reshape(512, D)
    chosen = pl.pallas_call(
        chosen_kernel,
        out_shape=jax.ShapeDtypeStruct((512, D), bf16),
        in_specs=[VM, VM],
        out_specs=HBM,
        scratch_shapes=[pltpu.VMEM((512, D), bf16), pltpu.SemaphoreType.DMA],
        compiler_params=params(20_000_000),
        cost_estimate=cost(0.6, 6),
        name="chosen",
    )(codes.reshape(512, 1), codebook)
    row = pltpu.VMEM((1, D), f32)
    tall = pltpu.VMEM((512, D), bf16)
    weights = [pltpu.VMEM((D, 3 * D), bf16), pltpu.VMEM((D, D), bf16)]
    sems = [
        pltpu.SemaphoreType.DMA((4,)),
        pltpu.SemaphoreType.DMA,
        pltpu.SemaphoreType.DMA((3, 4)),
        pltpu.SemaphoreType.DMA,
        pltpu.SemaphoreType.DMA((2,)),
    ]
    stream = pl.pallas_call(
        spatial_kernel,
        out_shape=jax.ShapeDtypeStruct((16, 8, 8, 512), bf16),
        in_specs=[HBM, HBM, SM, HBM, HBM],
        out_specs=HBM,
        scratch_shapes=[tall, row, *weights, tall, tall, pltpu.VMEM((16, 8, 8, 512), bf16), *sems],
        compiler_params=params(57_500_000),
        cost_estimate=cost(5, 10),
        name="spatial",
    )(x, gain_space.reshape(1, D), scale_space, qkv_space, out_space)
    stream = lax.all_to_all(stream.reshape(128, 8, 512), ("tm", "patch"), 0, 0, tiled=True)
    output = pl.pallas_call(
        temporal_kernel,
        out_shape=jax.ShapeDtypeStruct((512, D), bf16),
        in_specs=[HBM, HBM, SM, HBM, HBM],
        out_specs=HBM,
        scratch_shapes=[
            pltpu.VMEM((128, 8, 512), bf16), row, *weights, pltpu.VMEM((512, D), f32), tall, tall, tall, *sems,
        ],
        compiler_params=params(57_500_000),
        cost_estimate=cost(4, 10),
        name="temporal",
    )(stream, gain_time.reshape(1, D), scale_time, qkv_time, out_time)
    output = lax.all_to_all(output.reshape(16, 32, D), "tm", 0, 0, tiled=True)
    encoded, commitment = pl.pallas_call(
        final_kernel,
        out_shape=[jax.ShapeDtypeStruct((512, D), bf16)] * 2,
        in_specs=[VM, HBM],
        out_specs=[HBM, HBM],
        scratch_shapes=[pltpu.VMEM((512, D), bf16)] * 3 + [pltpu.SemaphoreType.DMA((9,))],
        input_output_aliases={1: 1},
        compiler_params=params(20_000_000),
        cost_estimate=cost(0.3, 4),
        name="final",
    )(output, chosen)
    return encoded.reshape(8, 64, D), commitment.reshape(8, 64, D)


def solution(mesh):
    rows = P("tm", "patch", None)
    return jax.shard_map(
        shards,
        mesh=mesh,
        in_specs=(rows, P("tm", "patch")) + (P(),) * 9,
        out_specs=(rows, rows),
        check_vma=False,
    )
```

```python
import functools
import math

import jax
import jax.numpy as jnp
from jax import lax
from jax.experimental import pallas as pl
from jax.experimental.pallas import tpu as pltpu
from jax.sharding import PartitionSpec as P

H = 16
HD = 64
D = 1024
GROUP = 256
PAIR = 128
ROWS = 256
LOG2E = math.log2(math.e)
f32 = jnp.float32
bf16 = jnp.bfloat16


def iota(shape, axis):
    return lax.broadcasted_iota(jnp.int32, shape, axis)


def same_head_mean():
    same = (iota((GROUP, GROUP), 0) // HD) == (iota((GROUP, GROUP), 1) // HD)
    return jnp.where(same, f32(1.0 / HD), f32(0.0)).astype(bf16)


def norm_rows(wide, gain):
    mean = jnp.mean(wide * wide, -1, keepdims=True)
    return (wide * lax.rsqrt(mean + 1e-5) * gain).astype(bf16)


def head_norm(block, averager):
    square = (block * block).astype(bf16)
    mean = jnp.dot(square, averager, preferred_element_type=f32)
    return block * lax.rsqrt(mean + 1e-6)


def scale_row(scale_ref, first_head):
    head = iota((1, GROUP), 1) // HD
    row = jnp.full((1, GROUP), scale_ref[first_head], f32)
    for h in range(1, GROUP // HD):
        row = jnp.where(head == h, scale_ref[first_head + h], row)
    return row * f32(LOG2E / HD)


def key_pair(key):
    low = iota(key.shape, 1) < HD
    zero = jnp.zeros_like(key)
    return jnp.concatenate([jnp.where(low, key, zero), jnp.where(low, zero, key)], 0)


def value_pair(value):
    low = iota(value.shape, 1) < HD
    zero = jnp.zeros_like(value)
    one = jnp.ones_like(value)
    first = jnp.concatenate([jnp.where(low, value, zero), jnp.where(low, one, zero)], 1)
    second = jnp.concatenate([jnp.where(low, zero, value), jnp.where(low, zero, one)], 1)
    return jnp.concatenate([first, second], 0)


def project(normed, qkv, scale_ref, averager, g):
    q, k, v = (
        jnp.dot(normed, qkv[:, part * D + g * GROUP : part * D + (g + 1) * GROUP], preferred_element_type=f32)
        for part in range(3)
    )
    q = (head_norm(q, averager) * scale_row(scale_ref, 4 * g)).astype(bf16)
    return q, head_norm(k, averager).astype(bf16), v.astype(bf16)


def weighted_mean(weights, values):
    o = jnp.dot(weights, values, preferred_element_type=f32)
    return (o[:, :PAIR] / o[:, PAIR:]).astype(bf16)


def logits(q, unit):
    lanes, rows, keys, _ = unit
    return lax.dot_general(q[rows, lanes], keys, (((1,), (1,)), ((), ())), preferred_element_type=f32)


def spatial_kernel(x, gain, scale_ref, qkv_hbm, out_hbm, o, qkv_buf, out_buf, normed, attn, sems, out_sem):
    out_copy = pltpu.make_async_copy(out_hbm, out_buf, out_sem)
    copies = [
        [
            pltpu.make_async_copy(
                qkv_hbm.at[:, pl.ds(part * D + start, count)],
                qkv_buf.at[:, pl.ds(part * D + start, count)],
                sems.at[n, part],
            )
            for part in range(3)
        ]
        for n, (start, count) in enumerate(((0, GROUP), (GROUP, D - GROUP)))
    ]
    for copy in copies[0]:
        copy.start()
    for n in range(4):
        rows = slice(128 * n, 128 * (n + 1))
        normed[rows, :] = norm_rows(x[rows, :].astype(f32), gain[...])
    averager = same_head_mean()
    for g in range(4):
        if g < 2:
            for copy in copies[g]:
                copy.wait()
        if g == 0:
            for copy in copies[1] + [out_copy]:
                copy.start()
        q, k, v = project(normed[...], qkv_buf, scale_ref, averager, g)
        units = []
        for pair in range(2):
            lanes = slice(pair * PAIR, (pair + 1) * PAIR)
            keys = key_pair(k[:, lanes])
            values = value_pair(v[:, lanes])
            for r in range(0, 512, ROWS):
                units.append((lanes, slice(r, r + ROWS), keys, values))
        s = logits(q, units[0])
        for n, (lanes, rows, keys, values) in enumerate(units):
            later = logits(q, units[n + 1]) if n + 1 < len(units) else None
            w = jnp.exp2(s).astype(bf16)
            ratio = weighted_mean(w, values)
            attn[rows, g * GROUP + lanes.start : g * GROUP + lanes.stop] = ratio
            s = later
    out_copy.wait()
    half = D // 2
    low = iota((1, 8, half), 1) < 4
    for n in range(2):
        rows = slice(256 * n, 256 * (n + 1))
        stream = x[rows, :].astype(f32) + jnp.dot(attn[rows, :], out_buf[...], preferred_element_type=f32)
        a = stream[:, :half].reshape(32, 8, half)
        b = stream[:, half:].reshape(32, 8, half)
        even = jnp.where(low, a, pltpu.roll(b, 4, 1)).astype(bf16)
        odd = jnp.where(low, pltpu.roll(a, 4, 1), b).astype(bf16)
        for j in range(4):
            runs = jnp.stack([even[8 * j : 8 * j + 8], odd[8 * j : 8 * j + 8]], 1)
            o[:, 4 * n + j] = runs.reshape(16, 8, half)


def temporal_kernel(
    x, gain, scale_ref, qkv_buf, out_buf, o_hbm, stream, normed, attn, o, o_sems
):
    half = D // 2
    one = f32(1.0)
    nil = f32(0.0)
    want = iota((128, 256), 0)
    source = (want & 31) * 8 + (want >> 5)
    first = jnp.where(iota((128, 256), 1) == source, one, nil).astype(bf16)
    second = jnp.where(iota((128, 256), 1) == source + 4, one, nil).astype(bf16)
    for b in range(4):
        recv = x[32 * b : 32 * (b + 1)].reshape(256, half)
        block = jnp.concatenate(
            [
                jnp.dot(first, recv, preferred_element_type=f32),
                jnp.dot(second, recv, preferred_element_type=f32),
            ],
            1,
        )
        ready = norm_rows(block, gain[...])
        for p in range(4):
            rows = slice(p * 128 + 32 * b, p * 128 + 32 * (b + 1))
            stream[rows, :] = block[32 * p : 32 * (p + 1)]
            normed[rows, :] = ready[32 * p : 32 * (p + 1)]
    averager = same_head_mean()
    causal = (iota((256, 256), 0) & 127) >= (iota((256, 256), 1) & 127)
    for g in range(4):
        q, k, v = project(normed[...], qkv_buf, scale_ref, averager, g)
        for pair in range(2):
            lanes = slice(pair * PAIR, (pair + 1) * PAIR)
            for p in range(0, 4, 2):
                one_rows = slice(p * 128, (p + 1) * 128)
                two_rows = slice((p + 1) * 128, (p + 2) * 128)
                blank = jnp.zeros((128, PAIR), bf16)
                queries = jnp.concatenate(
                    [
                        jnp.concatenate([q[one_rows, lanes], blank], 1),
                        jnp.concatenate([blank, q[two_rows, lanes]], 1),
                    ],
                    0,
                )
                keys = jnp.concatenate([key_pair(k[one_rows, lanes]), key_pair(k[two_rows, lanes])], 1)
                s = lax.dot_general(queries, keys, (((1,), (1,)), ((), ())), preferred_element_type=f32)
                w = jnp.where(causal, jnp.exp2(s), nil).astype(bf16)
                for n, rows in enumerate((one_rows, two_rows)):
                    ratio = weighted_mean(w[n * 128 : (n + 1) * 128], value_pair(v[rows, lanes]))
                    attn[rows, g * GROUP + lanes.start : g * GROUP + lanes.stop] = ratio
    want = iota((256, 256), 0)
    source = (want & 3) * 64 + (want >> 2)
    move = jnp.where(iota((256, 256), 1) == source, one, nil).astype(bf16)
    stores = []
    for b in range(2):
        pick = [slice(p * 128 + 64 * b, p * 128 + 64 * (b + 1)) for p in range(4)]
        mixed = jnp.concatenate([attn[rows, :] for rows in pick], 0)
        base = jnp.concatenate([stream[rows, :] for rows in pick], 0)
        output = (base + jnp.dot(mixed, out_buf[...], preferred_element_type=f32)).astype(bf16)
        rows = pl.ds(256 * b, 256)
        o[rows, :] = jnp.dot(move, output, preferred_element_type=f32).astype(bf16)
        store = pltpu.make_async_copy(o.at[rows, :], o_hbm.at[rows, :], o_sems.at[b])
        store.start()
        stores.append(store)
    for store in stores:
        store.wait()


def chosen_kernel(codes_ref, codebook_ref, o_hbm, rows, sem):
    hot = jnp.where(codes_ref[...] == iota((512, D), 1), f32(1.0), f32(0.0)).astype(bf16)
    rows[...] = jnp.dot(hot, codebook_ref[...], preferred_element_type=f32).astype(bf16)
    store = pltpu.make_async_copy(rows, o_hbm, sem)
    store.start()
    store.wait()


def final_kernel(x_ref, chosen_hbm, enc_hbm, com_hbm, chosen, enc, com, sems):
    load = pltpu.make_async_copy(chosen_hbm, chosen, sems.at[0])
    load.start()
    stores = []
    want = iota((128, 128), 0)
    source = ((want >> 2) & 15) * 8 + (want >> 6) * 4 + (want & 3)
    move = jnp.where(iota((128, 128), 1) == source, f32(1.0), f32(0.0)).astype(bf16)
    for n in range(4):
        rows = pl.ds(n * 128, 128)
        block = x_ref[:, 8 * n : 8 * (n + 1), :].reshape(128, D)
        output = jnp.dot(move, block, preferred_element_type=f32)
        enc[rows, :] = output.astype(bf16)
        store = pltpu.make_async_copy(enc.at[rows, :], enc_hbm.at[rows, :], sems.at[1 + 2 * n])
        store.start()
        stores.append(store)
        if n == 0:
            load.wait()
        com[rows, :] = (output - chosen[rows, :].astype(f32)).astype(bf16)
        store = pltpu.make_async_copy(com.at[rows, :], com_hbm.at[rows, :], sems.at[2 + 2 * n])
        store.start()
        stores.append(store)
    for store in stores:
        store.wait()


VM = pl.BlockSpec(memory_space=pltpu.VMEM)
HBM = pl.BlockSpec(memory_space=pltpu.HBM)
SM = pl.BlockSpec(memory_space=pltpu.SMEM)


def params(limit):
    return pltpu.CompilerParams(vmem_limit_bytes=limit)


def cost(gmac, mbytes):
    return pl.CostEstimate(flops=int(2e9 * gmac), bytes_accessed=int(1e6 * mbytes), transcendentals=0)


def shards(frames_in, codes, gain_space, qkv_space, out_space, scale_space, gain_time, qkv_time, out_time, scale_time, codebook):
    x = lax.all_to_all(frames_in, "patch", 0, 0, tiled=True).reshape(512, D)
    chosen = pl.pallas_call(
        chosen_kernel,
        out_shape=jax.ShapeDtypeStruct((512, D), bf16),
        in_specs=[VM, VM],
        out_specs=HBM,
        scratch_shapes=[pltpu.VMEM((512, D), bf16), pltpu.SemaphoreType.DMA],
        compiler_params=params(20_000_000),
        cost_estimate=cost(0.6, 6),
        name="chosen",
    )(codes.reshape(512, 1), codebook)
    tall = pltpu.VMEM((512, D), bf16)
    stream = pl.pallas_call(
        spatial_kernel,
        out_shape=jax.ShapeDtypeStruct((16, 8, 8, 512), bf16),
        in_specs=[VM, VM, SM, HBM, HBM],
        out_specs=VM,
        scratch_shapes=[
            pltpu.VMEM((D, 3 * D), bf16), pltpu.VMEM((D, D), bf16), tall, tall,
            pltpu.SemaphoreType.DMA((2, 3)), pltpu.SemaphoreType.DMA,
        ],
        compiler_params=params(52_500_000),
        cost_estimate=cost(5, 10),
        name="spatial",
    )(x, gain_space.reshape(1, D), scale_space, qkv_space, out_space)
    stream = lax.all_to_all(stream.reshape(128, 8, 512), ("tm", "patch"), 0, 0, tiled=True)
    output = pl.pallas_call(
        temporal_kernel,
        out_shape=jax.ShapeDtypeStruct((512, D), bf16),
        in_specs=[VM, VM, SM, VM, VM],
        out_specs=HBM,
        scratch_shapes=[pltpu.VMEM((512, D), f32), tall, tall, tall, pltpu.SemaphoreType.DMA((2,))],
        compiler_params=params(20_000_000),
        cost_estimate=cost(4, 10),
        name="temporal",
    )(stream, gain_time.reshape(1, D), scale_time, qkv_time, out_time)
    output = lax.all_to_all(output.reshape(16, 32, D), "tm", 0, 0, tiled=True)
    encoded, commitment = pl.pallas_call(
        final_kernel,
        out_shape=[jax.ShapeDtypeStruct((512, D), bf16)] * 2,
        in_specs=[VM, HBM],
        out_specs=[HBM, HBM],
        scratch_shapes=[pltpu.VMEM((512, D), bf16)] * 3 + [pltpu.SemaphoreType.DMA((9,))],
        input_output_aliases={1: 1},
        compiler_params=params(20_000_000),
        cost_estimate=cost(0.3, 4),
        name="final",
    )(output, chosen)
    return encoded.reshape(8, 64, D), commitment.reshape(8, 64, D)


def solution(mesh):
    rows = P("tm", "patch", None)
    return jax.shard_map(
        shards,
        mesh=mesh,
        in_specs=(rows, P("tm", "patch")) + (P(),) * 9,
        out_specs=(rows, rows),
        check_vma=False,
    )
```

```python
import functools
import math

import jax
import jax.numpy as jnp
from jax import lax
from jax.experimental import pallas as pl
from jax.experimental.pallas import tpu as pltpu
from jax.sharding import PartitionSpec as P

H = 16
HD = 64
D = 1024
GROUP = 256
PAIR = 128
ROWS = 256
LOG2E = math.log2(math.e)
f32 = jnp.float32
bf16 = jnp.bfloat16


def iota(shape, axis):
    return lax.broadcasted_iota(jnp.int32, shape, axis)


def same_head_mean():
    same = (iota((GROUP, GROUP), 0) // HD) == (iota((GROUP, GROUP), 1) // HD)
    return jnp.where(same, f32(1.0 / HD), f32(0.0)).astype(bf16)


def norm_rows(wide, gain):
    mean = jnp.mean(wide * wide, -1, keepdims=True)
    return (wide * lax.rsqrt(mean + 1e-5) * gain).astype(bf16)


def head_norm(block, averager):
    square = (block * block).astype(bf16)
    mean = jnp.dot(square, averager, preferred_element_type=f32)
    return block * lax.rsqrt(mean + 1e-6)


def scale_row(scale_ref, first_head):
    head = iota((1, GROUP), 1) // HD
    row = jnp.full((1, GROUP), scale_ref[first_head], f32)
    for h in range(1, GROUP // HD):
        row = jnp.where(head == h, scale_ref[first_head + h], row)
    return row * f32(LOG2E / HD)


def key_pair(key):
    low = iota(key.shape, 1) < HD
    zero = jnp.zeros_like(key)
    return jnp.concatenate([jnp.where(low, key, zero), jnp.where(low, zero, key)], 0)


def value_pair(value):
    low = iota(value.shape, 1) < HD
    zero = jnp.zeros_like(value)
    one = jnp.ones_like(value)
    first = jnp.concatenate([jnp.where(low, value, zero), jnp.where(low, one, zero)], 1)
    second = jnp.concatenate([jnp.where(low, zero, value), jnp.where(low, zero, one)], 1)
    return jnp.concatenate([first, second], 0)


def project(normed, qkv, scale_ref, averager, g):
    q, k, v = (
        jnp.dot(normed, qkv[:, part * D + g * GROUP : part * D + (g + 1) * GROUP], preferred_element_type=f32)
        for part in range(3)
    )
    q = (head_norm(q, averager) * scale_row(scale_ref, 4 * g)).astype(bf16)
    return q, head_norm(k, averager).astype(bf16), v.astype(bf16)


def weighted_mean(weights, values):
    o = jnp.dot(weights, values, preferred_element_type=f32)
    return (o[:, :PAIR] / o[:, PAIR:]).astype(bf16)


def logits(q, unit):
    lanes, rows, keys, _ = unit
    return lax.dot_general(q[rows, lanes], keys, (((1,), (1,)), ((), ())), preferred_element_type=f32)


def spatial_kernel(
    x, gain, scale_ref, codes, codebook, qkv_hbm, out_hbm, o, chosen_hbm,
    qkv_buf, out_buf, chosen, normed, attn, sems, out_sem, chosen_sem,
):
    out_copy = pltpu.make_async_copy(out_hbm, out_buf, out_sem)
    copies = [
        [
            pltpu.make_async_copy(
                qkv_hbm.at[:, pl.ds(part * D + start, count)],
                qkv_buf.at[:, pl.ds(part * D + start, count)],
                sems.at[n, part],
            )
            for part in range(3)
        ]
        for n, (start, count) in enumerate(((0, GROUP), (GROUP, D - GROUP)))
    ]
    for copy in copies[0]:
        copy.start()
    turned = codes[...].astype(f32).T
    for f in range(8):
        hot = jnp.where(turned[:, f : f + 1].astype(jnp.int32) == iota((64, D), 1), f32(1.0), f32(0.0)).astype(bf16)
        normed[64 * f : 64 * (f + 1), :] = hot
    chosen[...] = jnp.dot(normed[...], codebook[...], preferred_element_type=f32).astype(bf16)
    chosen_copy = pltpu.make_async_copy(chosen, chosen_hbm, chosen_sem)
    chosen_copy.start()
    for n in range(4):
        rows = slice(128 * n, 128 * (n + 1))
        normed[rows, :] = norm_rows(x[rows, :].astype(f32), gain[...])
    averager = same_head_mean()
    for g in range(4):
        if g < 2:
            for copy in copies[g]:
                copy.wait()
        if g == 0:
            for copy in copies[1] + [out_copy]:
                copy.start()
        q, k, v = project(normed[...], qkv_buf, scale_ref, averager, g)
        units = []
        for pair in range(2):
            lanes = slice(pair * PAIR, (pair + 1) * PAIR)
            keys = key_pair(k[:, lanes])
            values = value_pair(v[:, lanes])
            for r in range(0, 512, ROWS):
                units.append((lanes, slice(r, r + ROWS), keys, values))
        s = logits(q, units[0])
        for n, (lanes, rows, keys, values) in enumerate(units):
            later = logits(q, units[n + 1]) if n + 1 < len(units) else None
            w = jnp.exp2(s).astype(bf16)
            ratio = weighted_mean(w, values)
            attn[rows, g * GROUP + lanes.start : g * GROUP + lanes.stop] = ratio
            s = later
    out_copy.wait()
    half = D // 2
    low = iota((1, 8, half), 1) < 4
    for n in range(2):
        rows = slice(256 * n, 256 * (n + 1))
        stream = x[rows, :].astype(f32) + jnp.dot(attn[rows, :], out_buf[...], preferred_element_type=f32)
        a = stream[:, :half].reshape(32, 8, half)
        b = stream[:, half:].reshape(32, 8, half)
        even = jnp.where(low, a, pltpu.roll(b, 4, 1)).astype(bf16)
        odd = jnp.where(low, pltpu.roll(a, 4, 1), b).astype(bf16)
        for j in range(4):
            runs = jnp.stack([even[8 * j : 8 * j + 8], odd[8 * j : 8 * j + 8]], 1)
            o[:, 4 * n + j] = runs.reshape(16, 8, half)
    chosen_copy.wait()


def temporal_kernel(
    x, gain, scale_ref, qkv_buf, out_buf, o_hbm, stream, normed, attn, o, o_sems
):
    half = D // 2
    one = f32(1.0)
    nil = f32(0.0)
    want = iota((128, 256), 0)
    source = (want & 31) * 8 + (want >> 5)
    first = jnp.where(iota((128, 256), 1) == source, one, nil).astype(bf16)
    second = jnp.where(iota((128, 256), 1) == source + 4, one, nil).astype(bf16)
    for b in range(4):
        recv = x[32 * b : 32 * (b + 1)].reshape(256, half)
        block = jnp.concatenate(
            [
                jnp.dot(first, recv, preferred_element_type=f32),
                jnp.dot(second, recv, preferred_element_type=f32),
            ],
            1,
        )
        ready = norm_rows(block, gain[...])
        for p in range(4):
            rows = slice(p * 128 + 32 * b, p * 128 + 32 * (b + 1))
            stream[rows, :] = block[32 * p : 32 * (p + 1)]
            normed[rows, :] = ready[32 * p : 32 * (p + 1)]
    averager = same_head_mean()
    causal = (iota((256, 256), 0) & 127) >= (iota((256, 256), 1) & 127)
    for g in range(4):
        q, k, v = project(normed[...], qkv_buf, scale_ref, averager, g)
        for pair in range(2):
            lanes = slice(pair * PAIR, (pair + 1) * PAIR)
            for p in range(0, 4, 2):
                one_rows = slice(p * 128, (p + 1) * 128)
                two_rows = slice((p + 1) * 128, (p + 2) * 128)
                blank = jnp.zeros((128, PAIR), bf16)
                queries = jnp.concatenate(
                    [
                        jnp.concatenate([q[one_rows, lanes], blank], 1),
                        jnp.concatenate([blank, q[two_rows, lanes]], 1),
                    ],
                    0,
                )
                keys = jnp.concatenate([key_pair(k[one_rows, lanes]), key_pair(k[two_rows, lanes])], 1)
                s = lax.dot_general(queries, keys, (((1,), (1,)), ((), ())), preferred_element_type=f32)
                w = jnp.where(causal, jnp.exp2(s), nil).astype(bf16)
                for n, rows in enumerate((one_rows, two_rows)):
                    ratio = weighted_mean(w[n * 128 : (n + 1) * 128], value_pair(v[rows, lanes]))
                    attn[rows, g * GROUP + lanes.start : g * GROUP + lanes.stop] = ratio
    want = iota((256, 256), 0)
    source = (want & 3) * 64 + (want >> 2)
    move = jnp.where(iota((256, 256), 1) == source, one, nil).astype(bf16)
    stores = []
    for b in range(2):
        pick = [slice(p * 128 + 64 * b, p * 128 + 64 * (b + 1)) for p in range(4)]
        mixed = jnp.concatenate([attn[rows, :] for rows in pick], 0)
        base = jnp.concatenate([stream[rows, :] for rows in pick], 0)
        output = (base + jnp.dot(mixed, out_buf[...], preferred_element_type=f32)).astype(bf16)
        rows = pl.ds(256 * b, 256)
        o[rows, :] = jnp.dot(move, output, preferred_element_type=f32).astype(bf16)
        store = pltpu.make_async_copy(o.at[rows, :], o_hbm.at[rows, :], o_sems.at[b])
        store.start()
        stores.append(store)
    for store in stores:
        store.wait()


def final_kernel(x_ref, chosen_hbm, enc_hbm, com_hbm, chosen, enc, com, sems):
    load = pltpu.make_async_copy(chosen_hbm, chosen, sems.at[0])
    load.start()
    stores = []
    want = iota((128, 128), 0)
    source = ((want >> 2) & 15) * 8 + (want >> 6) * 4 + (want & 3)
    move = jnp.where(iota((128, 128), 1) == source, f32(1.0), f32(0.0)).astype(bf16)
    outputs = []
    for n in range(4):
        rows = pl.ds(n * 128, 128)
        block = x_ref[:, 8 * n : 8 * (n + 1), :].reshape(128, D)
        output = jnp.dot(move, block, preferred_element_type=f32)
        outputs.append(output)
        enc[rows, :] = output.astype(bf16)
        store = pltpu.make_async_copy(enc.at[rows, :], enc_hbm.at[rows, :], sems.at[1 + n])
        store.start()
        stores.append(store)
    load.wait()
    for n, output in enumerate(outputs):
        rows = pl.ds(n * 128, 128)
        com[rows, :] = (output - chosen[rows, :].astype(f32)).astype(bf16)
        store = pltpu.make_async_copy(com.at[rows, :], com_hbm.at[rows, :], sems.at[5 + n])
        store.start()
        stores.append(store)
    for store in stores:
        store.wait()


VM = pl.BlockSpec(memory_space=pltpu.VMEM)
HBM = pl.BlockSpec(memory_space=pltpu.HBM)
SM = pl.BlockSpec(memory_space=pltpu.SMEM)


def params(limit):
    return pltpu.CompilerParams(vmem_limit_bytes=limit)


def cost(gmac, mbytes):
    return pl.CostEstimate(flops=int(2e9 * gmac), bytes_accessed=int(1e6 * mbytes), transcendentals=0)


def shards(frames_in, codes, gain_space, qkv_space, out_space, scale_space, gain_time, qkv_time, out_time, scale_time, codebook):
    x = lax.all_to_all(frames_in, "patch", 0, 0, tiled=True).reshape(512, D)
    tall = pltpu.VMEM((512, D), bf16)
    stream, chosen = pl.pallas_call(
        spatial_kernel,
        out_shape=[jax.ShapeDtypeStruct((16, 8, 8, 512), bf16), jax.ShapeDtypeStruct((512, D), bf16)],
        in_specs=[VM, VM, SM, VM, VM, HBM, HBM],
        out_specs=[VM, HBM],
        scratch_shapes=[
            pltpu.VMEM((D, 3 * D), bf16), pltpu.VMEM((D, D), bf16), tall, tall, tall,
            pltpu.SemaphoreType.DMA((2, 3)), pltpu.SemaphoreType.DMA, pltpu.SemaphoreType.DMA,
        ],
        compiler_params=params(51_500_000),
        cost_estimate=cost(5, 10),
        name="spatial",
    )(x, gain_space.reshape(1, D), scale_space, codes, codebook, qkv_space, out_space)
    stream = lax.all_to_all(stream.reshape(128, 8, 512), ("tm", "patch"), 0, 0, tiled=True)
    output = pl.pallas_call(
        temporal_kernel,
        out_shape=jax.ShapeDtypeStruct((512, D), bf16),
        in_specs=[VM, VM, SM, VM, VM],
        out_specs=HBM,
        scratch_shapes=[pltpu.VMEM((512, D), f32), tall, tall, tall, pltpu.SemaphoreType.DMA((2,))],
        compiler_params=params(20_000_000),
        cost_estimate=cost(4, 10),
        name="temporal",
    )(stream, gain_time.reshape(1, D), scale_time, qkv_time, out_time)
    output = lax.all_to_all(output.reshape(16, 32, D), "tm", 0, 0, tiled=True)
    encoded, commitment = pl.pallas_call(
        final_kernel,
        out_shape=[jax.ShapeDtypeStruct((512, D), bf16)] * 2,
        in_specs=[VM, HBM],
        out_specs=[HBM, HBM],
        scratch_shapes=[pltpu.VMEM((512, D), bf16)] * 3 + [pltpu.SemaphoreType.DMA((9,))],
        input_output_aliases={1: 1},
        compiler_params=params(20_000_000),
        cost_estimate=cost(0.3, 4),
        name="final",
    )(output, chosen)
    return encoded.reshape(8, 64, D), commitment.reshape(8, 64, D)


def solution(mesh):
    rows = P("tm", "patch", None)
    return jax.shard_map(
        shards,
        mesh=mesh,
        in_specs=(rows, P("tm", "patch")) + (P(),) * 9,
        out_specs=(rows, rows),
        check_vma=False,
    )
```

```python
import functools
import math

import jax
import jax.numpy as jnp
from jax import lax
from jax.experimental import pallas as pl
from jax.experimental.pallas import tpu as pltpu
from jax.sharding import PartitionSpec as P

H = 16
HD = 64
D = 1024
GROUP = 256
PAIR = 128
ROWS = 256
LOG2E = math.log2(math.e)
f32 = jnp.float32
bf16 = jnp.bfloat16


def iota(shape, axis):
    return lax.broadcasted_iota(jnp.int32, shape, axis)


def same_head_mean():
    same = (iota((GROUP, GROUP), 0) // HD) == (iota((GROUP, GROUP), 1) // HD)
    return jnp.where(same, f32(1.0 / HD), f32(0.0)).astype(bf16)


def norm_rows(wide, gain):
    mean = jnp.mean(wide * wide, -1, keepdims=True)
    return (wide * lax.rsqrt(mean + 1e-5) * gain).astype(bf16)


def head_norm(block, averager):
    square = (block * block).astype(bf16)
    mean = jnp.dot(square, averager, preferred_element_type=f32)
    return block * lax.rsqrt(mean + 1e-6)


def scale_row(scale_ref, first_head):
    head = iota((1, GROUP), 1) // HD
    row = jnp.full((1, GROUP), scale_ref[first_head], f32)
    for h in range(1, GROUP // HD):
        row = jnp.where(head == h, scale_ref[first_head + h], row)
    return row * f32(LOG2E / HD)


def key_pair(key):
    low = iota(key.shape, 1) < HD
    zero = jnp.zeros_like(key)
    return jnp.concatenate([jnp.where(low, key, zero), jnp.where(low, zero, key)], 0)


def value_pair(value):
    low = iota(value.shape, 1) < HD
    zero = jnp.zeros_like(value)
    one = jnp.ones_like(value)
    first = jnp.concatenate([jnp.where(low, value, zero), jnp.where(low, one, zero)], 1)
    second = jnp.concatenate([jnp.where(low, zero, value), jnp.where(low, zero, one)], 1)
    return jnp.concatenate([first, second], 0)


def project(normed, qkv, scale_ref, averager, g):
    q, k, v = (
        jnp.dot(normed, qkv[:, part * D + g * GROUP : part * D + (g + 1) * GROUP], preferred_element_type=f32)
        for part in range(3)
    )
    q = (head_norm(q, averager) * scale_row(scale_ref, 4 * g)).astype(bf16)
    return q, head_norm(k, averager).astype(bf16), v.astype(bf16)


def weighted_mean(weights, values):
    o = jnp.dot(weights, values, preferred_element_type=f32)
    return (o[:, :PAIR] / o[:, PAIR:]).astype(bf16)


def logits(q, unit):
    lanes, rows, keys, _ = unit
    return lax.dot_general(q[rows, lanes], keys, (((1,), (1,)), ((), ())), preferred_element_type=f32)


def spatial_kernel(
    x, gain, scale_ref, qkv_hbm, out_hbm, o, qkv_buf, out_buf, normed, attn, sems, out_sem
):
    out_copy = pltpu.make_async_copy(out_hbm, out_buf, out_sem)
    copies = [
        [
            pltpu.make_async_copy(
                qkv_hbm.at[:, pl.ds(part * D + start, count)],
                qkv_buf.at[:, pl.ds(part * D + start, count)],
                sems.at[n, part],
            )
            for part in range(3)
        ]
        for n, (start, count) in enumerate(((0, GROUP), (GROUP, D - GROUP)))
    ]
    for copy in copies[0]:
        copy.start()
    for n in range(4):
        rows = slice(128 * n, 128 * (n + 1))
        normed[rows, :] = norm_rows(x[rows, :].astype(f32), gain[...])
    averager = same_head_mean()
    for g in range(4):
        if g < 2:
            for copy in copies[g]:
                copy.wait()
        if g == 0:
            for copy in copies[1] + [out_copy]:
                copy.start()
        q, k, v = project(normed[...], qkv_buf, scale_ref, averager, g)
        units = []
        for pair in range(2):
            lanes = slice(pair * PAIR, (pair + 1) * PAIR)
            keys = key_pair(k[:, lanes])
            values = value_pair(v[:, lanes])
            for r in range(0, 512, ROWS):
                units.append((lanes, slice(r, r + ROWS), keys, values))
        s = logits(q, units[0])
        for n, (lanes, rows, keys, values) in enumerate(units):
            later = logits(q, units[n + 1]) if n + 1 < len(units) else None
            w = jnp.exp2(s).astype(bf16)
            ratio = weighted_mean(w, values)
            attn[rows, g * GROUP + lanes.start : g * GROUP + lanes.stop] = ratio
            s = later
    out_copy.wait()
    half = D // 2
    low = iota((1, 8, half), 1) < 4
    for n in range(2):
        rows = slice(256 * n, 256 * (n + 1))
        stream = x[rows, :].astype(f32) + jnp.dot(attn[rows, :], out_buf[...], preferred_element_type=f32)
        a = stream[:, :half].reshape(32, 8, half)
        b = stream[:, half:].reshape(32, 8, half)
        even = jnp.where(low, a, pltpu.roll(b, 4, 1)).astype(bf16)
        odd = jnp.where(low, pltpu.roll(a, 4, 1), b).astype(bf16)
        for j in range(4):
            runs = jnp.stack([even[8 * j : 8 * j + 8], odd[8 * j : 8 * j + 8]], 1)
            o[:, 4 * n + j] = runs.reshape(16, 8, half)


def temporal_kernel(
    x, gain, scale_ref, qkv_buf, out_buf, codes, codebook, o_hbm, chosen_hbm,
    stream, normed, attn, o, chosen, o_sems, chosen_sem,
):
    turned = codes[...].astype(f32).T
    for f in range(8):
        hot = jnp.where(turned[:, f : f + 1].astype(jnp.int32) == iota((64, D), 1), f32(1.0), f32(0.0)).astype(bf16)
        attn[64 * f : 64 * (f + 1), :] = hot
    chosen[...] = jnp.dot(attn[...], codebook[...], preferred_element_type=f32).astype(bf16)
    chosen_copy = pltpu.make_async_copy(chosen, chosen_hbm, chosen_sem)
    chosen_copy.start()
    half = D // 2
    one = f32(1.0)
    nil = f32(0.0)
    want = iota((128, 256), 0)
    source = (want & 31) * 8 + (want >> 5)
    first = jnp.where(iota((128, 256), 1) == source, one, nil).astype(bf16)
    second = jnp.where(iota((128, 256), 1) == source + 4, one, nil).astype(bf16)
    for b in range(4):
        recv = x[32 * b : 32 * (b + 1)].reshape(256, half)
        block = jnp.concatenate(
            [
                jnp.dot(first, recv, preferred_element_type=f32),
                jnp.dot(second, recv, preferred_element_type=f32),
            ],
            1,
        )
        ready = norm_rows(block, gain[...])
        for p in range(4):
            rows = slice(p * 128 + 32 * b, p * 128 + 32 * (b + 1))
            stream[rows, :] = block[32 * p : 32 * (p + 1)]
            normed[rows, :] = ready[32 * p : 32 * (p + 1)]
    averager = same_head_mean()
    causal = (iota((256, 256), 0) & 127) >= (iota((256, 256), 1) & 127)
    for g in range(4):
        q, k, v = project(normed[...], qkv_buf, scale_ref, averager, g)
        for pair in range(2):
            lanes = slice(pair * PAIR, (pair + 1) * PAIR)
            for p in range(0, 4, 2):
                one_rows = slice(p * 128, (p + 1) * 128)
                two_rows = slice((p + 1) * 128, (p + 2) * 128)
                blank = jnp.zeros((128, PAIR), bf16)
                queries = jnp.concatenate(
                    [
                        jnp.concatenate([q[one_rows, lanes], blank], 1),
                        jnp.concatenate([blank, q[two_rows, lanes]], 1),
                    ],
                    0,
                )
                keys = jnp.concatenate([key_pair(k[one_rows, lanes]), key_pair(k[two_rows, lanes])], 1)
                s = lax.dot_general(queries, keys, (((1,), (1,)), ((), ())), preferred_element_type=f32)
                w = jnp.where(causal, jnp.exp2(s), nil).astype(bf16)
                for n, rows in enumerate((one_rows, two_rows)):
                    ratio = weighted_mean(w[n * 128 : (n + 1) * 128], value_pair(v[rows, lanes]))
                    attn[rows, g * GROUP + lanes.start : g * GROUP + lanes.stop] = ratio
    want = iota((256, 256), 0)
    source = (want & 3) * 64 + (want >> 2)
    move = jnp.where(iota((256, 256), 1) == source, one, nil).astype(bf16)
    stores = []
    for b in range(2):
        pick = [slice(p * 128 + 64 * b, p * 128 + 64 * (b + 1)) for p in range(4)]
        mixed = jnp.concatenate([attn[rows, :] for rows in pick], 0)
        base = jnp.concatenate([stream[rows, :] for rows in pick], 0)
        output = (base + jnp.dot(mixed, out_buf[...], preferred_element_type=f32)).astype(bf16)
        rows = pl.ds(256 * b, 256)
        o[rows, :] = jnp.dot(move, output, preferred_element_type=f32).astype(bf16)
        store = pltpu.make_async_copy(o.at[rows, :], o_hbm.at[rows, :], o_sems.at[b])
        store.start()
        stores.append(store)
    for store in stores:
        store.wait()
    chosen_copy.wait()


def final_kernel(x_ref, chosen_hbm, enc_hbm, com_hbm, chosen, enc, com, sems):
    load = pltpu.make_async_copy(chosen_hbm, chosen, sems.at[0])
    load.start()
    stores = []
    want = iota((128, 128), 0)
    source = ((want >> 2) & 15) * 8 + (want >> 6) * 4 + (want & 3)
    move = jnp.where(iota((128, 128), 1) == source, f32(1.0), f32(0.0)).astype(bf16)
    outputs = []
    for n in range(4):
        rows = pl.ds(n * 128, 128)
        block = x_ref[:, 8 * n : 8 * (n + 1), :].reshape(128, D)
        output = jnp.dot(move, block, preferred_element_type=f32)
        outputs.append(output)
        enc[rows, :] = output.astype(bf16)
        store = pltpu.make_async_copy(enc.at[rows, :], enc_hbm.at[rows, :], sems.at[1 + n])
        store.start()
        stores.append(store)
    load.wait()
    for n, output in enumerate(outputs):
        rows = pl.ds(n * 128, 128)
        com[rows, :] = (output - chosen[rows, :].astype(f32)).astype(bf16)
        store = pltpu.make_async_copy(com.at[rows, :], com_hbm.at[rows, :], sems.at[5 + n])
        store.start()
        stores.append(store)
    for store in stores:
        store.wait()


VM = pl.BlockSpec(memory_space=pltpu.VMEM)
HBM = pl.BlockSpec(memory_space=pltpu.HBM)
SM = pl.BlockSpec(memory_space=pltpu.SMEM)


def params(limit):
    return pltpu.CompilerParams(vmem_limit_bytes=limit)


def cost(gmac, mbytes):
    return pl.CostEstimate(flops=int(2e9 * gmac), bytes_accessed=int(1e6 * mbytes), transcendentals=0)


def shards(frames_in, codes, gain_space, qkv_space, out_space, scale_space, gain_time, qkv_time, out_time, scale_time, codebook):
    x = lax.all_to_all(frames_in, "patch", 0, 0, tiled=True).reshape(512, D)
    tall = pltpu.VMEM((512, D), bf16)
    stream = pl.pallas_call(
        spatial_kernel,
        out_shape=jax.ShapeDtypeStruct((16, 8, 8, 512), bf16),
        in_specs=[VM, VM, SM, HBM, HBM],
        out_specs=VM,
        scratch_shapes=[
            pltpu.VMEM((D, 3 * D), bf16), pltpu.VMEM((D, D), bf16), tall, tall,
            pltpu.SemaphoreType.DMA((2, 3)), pltpu.SemaphoreType.DMA,
        ],
        compiler_params=params(52_500_000),
        cost_estimate=cost(5, 10),
        name="spatial",
    )(x, gain_space.reshape(1, D), scale_space, qkv_space, out_space)
    stream = lax.all_to_all(stream.reshape(128, 8, 512), ("tm", "patch"), 0, 0, tiled=True)
    output, chosen = pl.pallas_call(
        temporal_kernel,
        out_shape=[jax.ShapeDtypeStruct((512, D), bf16)] * 2,
        in_specs=[VM, VM, SM, VM, VM, VM, VM],
        out_specs=[HBM, HBM],
        scratch_shapes=[
            pltpu.VMEM((512, D), f32), tall, tall, tall, tall,
            pltpu.SemaphoreType.DMA((2,)), pltpu.SemaphoreType.DMA,
        ],
        compiler_params=params(20_000_000),
        cost_estimate=cost(4, 10),
        name="temporal",
    )(stream, gain_time.reshape(1, D), scale_time, qkv_time, out_time, codes, codebook)
    output = lax.all_to_all(output.reshape(16, 32, D), "tm", 0, 0, tiled=True)
    encoded, commitment = pl.pallas_call(
        final_kernel,
        out_shape=[jax.ShapeDtypeStruct((512, D), bf16)] * 2,
        in_specs=[VM, HBM],
        out_specs=[HBM, HBM],
        scratch_shapes=[pltpu.VMEM((512, D), bf16)] * 3 + [pltpu.SemaphoreType.DMA((9,))],
        input_output_aliases={1: 1},
        compiler_params=params(20_000_000),
        cost_estimate=cost(0.3, 4),
        name="final",
    )(output, chosen)
    return encoded.reshape(8, 64, D), commitment.reshape(8, 64, D)


def solution(mesh):
    rows = P("tm", "patch", None)
    return jax.shard_map(
        shards,
        mesh=mesh,
        in_specs=(rows, P("tm", "patch")) + (P(),) * 9,
        out_specs=(rows, rows),
        check_vma=False,
    )
```

```python
import functools
import math

import jax
import jax.numpy as jnp
from jax import lax
from jax.experimental import pallas as pl
from jax.experimental.pallas import tpu as pltpu
from jax.sharding import PartitionSpec as P

H = 16
HD = 64
D = 1024
GROUP = 256
PAIR = 128
ROWS = 256
LOG2E = math.log2(math.e)
f32 = jnp.float32
bf16 = jnp.bfloat16


def iota(shape, axis):
    return lax.broadcasted_iota(jnp.int32, shape, axis)


def same_head_mean():
    same = (iota((GROUP, GROUP), 0) // HD) == (iota((GROUP, GROUP), 1) // HD)
    return jnp.where(same, f32(1.0 / HD), f32(0.0)).astype(bf16)


def norm_rows(wide, gain):
    mean = jnp.mean(wide * wide, -1, keepdims=True)
    return (wide * lax.rsqrt(mean + 1e-5) * gain).astype(bf16)


def head_norm(block, averager):
    square = (block * block).astype(bf16)
    mean = jnp.dot(square, averager, preferred_element_type=f32)
    return block * lax.rsqrt(mean + 1e-6)


def scale_row(scale_ref, first_head):
    head = iota((1, GROUP), 1) // HD
    row = jnp.full((1, GROUP), scale_ref[first_head], f32)
    for h in range(1, GROUP // HD):
        row = jnp.where(head == h, scale_ref[first_head + h], row)
    return row * f32(LOG2E / HD)


def key_pair(key):
    low = iota(key.shape, 1) < HD
    zero = jnp.zeros_like(key)
    return jnp.concatenate([jnp.where(low, key, zero), jnp.where(low, zero, key)], 0)


def value_pair(value):
    low = iota(value.shape, 1) < HD
    zero = jnp.zeros_like(value)
    one = jnp.ones_like(value)
    first = jnp.concatenate([jnp.where(low, value, zero), jnp.where(low, one, zero)], 1)
    second = jnp.concatenate([jnp.where(low, zero, value), jnp.where(low, zero, one)], 1)
    return jnp.concatenate([first, second], 0)


def project(normed, qkv, scale_ref, averager, g):
    q, k, v = (
        jnp.dot(normed, qkv[:, part * D + g * GROUP : part * D + (g + 1) * GROUP], preferred_element_type=f32)
        for part in range(3)
    )
    q = (head_norm(q, averager) * scale_row(scale_ref, 4 * g)).astype(bf16)
    return q, head_norm(k, averager).astype(bf16), v.astype(bf16)


def weighted_mean(weights, values):
    o = jnp.dot(weights, values, preferred_element_type=f32)
    return (o[:, :PAIR] / o[:, PAIR:]).astype(bf16)


def logits(q, unit):
    lanes, rows, keys, _ = unit
    return lax.dot_general(q[rows, lanes], keys, (((1,), (1,)), ((), ())), preferred_element_type=f32)


def spatial_kernel(
    x, gain, scale_ref, qkv_hbm, out_hbm, o, qkv_buf, out_buf, normed, attn, sems, out_sem
):
    out_copy = pltpu.make_async_copy(out_hbm, out_buf, out_sem)
    copies = [
        [
            pltpu.make_async_copy(
                qkv_hbm.at[:, pl.ds(part * D + start, count)],
                qkv_buf.at[:, pl.ds(part * D + start, count)],
                sems.at[n, part],
            )
            for part in range(3)
        ]
        for n, (start, count) in enumerate(((0, GROUP), (GROUP, D - GROUP)))
    ]
    for copy in copies[0]:
        copy.start()
    for n in range(4):
        rows = slice(128 * n, 128 * (n + 1))
        normed[rows, :] = norm_rows(x[rows, :].astype(f32), gain[...])
    averager = same_head_mean()
    for g in range(4):
        if g < 2:
            for copy in copies[g]:
                copy.wait()
        if g == 0:
            for copy in copies[1] + [out_copy]:
                copy.start()
        q, k, v = project(normed[...], qkv_buf, scale_ref, averager, g)
        units = []
        for pair in range(2):
            lanes = slice(pair * PAIR, (pair + 1) * PAIR)
            keys = key_pair(k[:, lanes])
            values = value_pair(v[:, lanes])
            for r in range(0, 512, ROWS):
                units.append((lanes, slice(r, r + ROWS), keys, values))
        s = logits(q, units[0])
        for n, (lanes, rows, keys, values) in enumerate(units):
            later = logits(q, units[n + 1]) if n + 1 < len(units) else None
            w = jnp.exp2(s).astype(bf16)
            ratio = weighted_mean(w, values)
            attn[rows, g * GROUP + lanes.start : g * GROUP + lanes.stop] = ratio
            s = later
    out_copy.wait()
    half = D // 2
    low = iota((1, 8, half), 1) < 4
    for n in range(2):
        rows = slice(256 * n, 256 * (n + 1))
        stream = x[rows, :].astype(f32) + jnp.dot(attn[rows, :], out_buf[...], preferred_element_type=f32)
        a = stream[:, :half].reshape(32, 8, half)
        b = stream[:, half:].reshape(32, 8, half)
        even = jnp.where(low, a, pltpu.roll(b, 4, 1)).astype(bf16)
        odd = jnp.where(low, pltpu.roll(a, 4, 1), b).astype(bf16)
        for j in range(4):
            runs = jnp.stack([even[8 * j : 8 * j + 8], odd[8 * j : 8 * j + 8]], 1)
            o[:, 4 * n + j] = runs.reshape(16, 8, half)


def temporal_kernel(
    x, gain, scale_ref, qkv_buf, out_buf, codes, codebook, o_hbm, chosen_hbm,
    stream, normed, attn, o, chosen, o_sems, chosen_sem,
):
    turned = codes[...].astype(f32).T
    for f in range(8):
        hot = jnp.where(turned[:, f : f + 1].astype(jnp.int32) == iota((64, D), 1), f32(1.0), f32(0.0)).astype(bf16)
        o[64 * f : 64 * (f + 1), :] = hot
    half = D // 2
    one = f32(1.0)
    nil = f32(0.0)
    want = iota((128, 256), 0)
    source = (want & 31) * 8 + (want >> 5)
    first = jnp.where(iota((128, 256), 1) == source, one, nil).astype(bf16)
    second = jnp.where(iota((128, 256), 1) == source + 4, one, nil).astype(bf16)
    for b in range(4):
        recv = x[32 * b : 32 * (b + 1)].reshape(256, half)
        block = jnp.concatenate(
            [
                jnp.dot(first, recv, preferred_element_type=f32),
                jnp.dot(second, recv, preferred_element_type=f32),
            ],
            1,
        )
        ready = norm_rows(block, gain[...])
        for p in range(4):
            rows = slice(p * 128 + 32 * b, p * 128 + 32 * (b + 1))
            stream[rows, :] = block[32 * p : 32 * (p + 1)]
            normed[rows, :] = ready[32 * p : 32 * (p + 1)]
    averager = same_head_mean()
    causal = (iota((256, 256), 0) & 127) >= (iota((256, 256), 1) & 127)
    for g in range(4):
        q, k, v = project(normed[...], qkv_buf, scale_ref, averager, g)
        part = slice(g * GROUP, (g + 1) * GROUP)
        chosen[:, part] = jnp.dot(o[...], codebook[:, part], preferred_element_type=f32).astype(bf16)
        for pair in range(2):
            lanes = slice(pair * PAIR, (pair + 1) * PAIR)
            for p in range(0, 4, 2):
                one_rows = slice(p * 128, (p + 1) * 128)
                two_rows = slice((p + 1) * 128, (p + 2) * 128)
                blank = jnp.zeros((128, PAIR), bf16)
                queries = jnp.concatenate(
                    [
                        jnp.concatenate([q[one_rows, lanes], blank], 1),
                        jnp.concatenate([blank, q[two_rows, lanes]], 1),
                    ],
                    0,
                )
                keys = jnp.concatenate([key_pair(k[one_rows, lanes]), key_pair(k[two_rows, lanes])], 1)
                s = lax.dot_general(queries, keys, (((1,), (1,)), ((), ())), preferred_element_type=f32)
                w = jnp.where(causal, jnp.exp2(s), nil).astype(bf16)
                for n, rows in enumerate((one_rows, two_rows)):
                    ratio = weighted_mean(w[n * 128 : (n + 1) * 128], value_pair(v[rows, lanes]))
                    attn[rows, g * GROUP + lanes.start : g * GROUP + lanes.stop] = ratio
    chosen_copy = pltpu.make_async_copy(chosen, chosen_hbm, chosen_sem)
    chosen_copy.start()
    want = iota((256, 256), 0)
    source = (want & 3) * 64 + (want >> 2)
    move = jnp.where(iota((256, 256), 1) == source, one, nil).astype(bf16)
    stores = []
    for b in range(2):
        pick = [slice(p * 128 + 64 * b, p * 128 + 64 * (b + 1)) for p in range(4)]
        mixed = jnp.concatenate([attn[rows, :] for rows in pick], 0)
        base = jnp.concatenate([stream[rows, :] for rows in pick], 0)
        output = (base + jnp.dot(mixed, out_buf[...], preferred_element_type=f32)).astype(bf16)
        rows = pl.ds(256 * b, 256)
        o[rows, :] = jnp.dot(move, output, preferred_element_type=f32).astype(bf16)
        store = pltpu.make_async_copy(o.at[rows, :], o_hbm.at[rows, :], o_sems.at[b])
        store.start()
        stores.append(store)
    for store in stores:
        store.wait()
    chosen_copy.wait()


def final_kernel(x_ref, chosen_hbm, enc_hbm, com_hbm, chosen, enc, com, sems):
    load = pltpu.make_async_copy(chosen_hbm, chosen, sems.at[0])
    load.start()
    stores = []
    want = iota((128, 128), 0)
    source = ((want >> 2) & 15) * 8 + (want >> 6) * 4 + (want & 3)
    move = jnp.where(iota((128, 128), 1) == source, f32(1.0), f32(0.0)).astype(bf16)
    outputs = []
    for n in range(4):
        rows = pl.ds(n * 128, 128)
        block = x_ref[:, 8 * n : 8 * (n + 1), :].reshape(128, D)
        output = jnp.dot(move, block, preferred_element_type=f32)
        outputs.append(output)
        enc[rows, :] = output.astype(bf16)
        store = pltpu.make_async_copy(enc.at[rows, :], enc_hbm.at[rows, :], sems.at[1 + n])
        store.start()
        stores.append(store)
    load.wait()
    for n, output in enumerate(outputs):
        rows = pl.ds(n * 128, 128)
        com[rows, :] = (output - chosen[rows, :].astype(f32)).astype(bf16)
        store = pltpu.make_async_copy(com.at[rows, :], com_hbm.at[rows, :], sems.at[5 + n])
        store.start()
        stores.append(store)
    for store in stores:
        store.wait()


VM = pl.BlockSpec(memory_space=pltpu.VMEM)
HBM = pl.BlockSpec(memory_space=pltpu.HBM)
SM = pl.BlockSpec(memory_space=pltpu.SMEM)


def params(limit):
    return pltpu.CompilerParams(vmem_limit_bytes=limit)


def cost(gmac, mbytes):
    return pl.CostEstimate(flops=int(2e9 * gmac), bytes_accessed=int(1e6 * mbytes), transcendentals=0)


def shards(frames_in, codes, gain_space, qkv_space, out_space, scale_space, gain_time, qkv_time, out_time, scale_time, codebook):
    x = lax.all_to_all(frames_in, "patch", 0, 0, tiled=True).reshape(512, D)
    tall = pltpu.VMEM((512, D), bf16)
    stream = pl.pallas_call(
        spatial_kernel,
        out_shape=jax.ShapeDtypeStruct((16, 8, 8, 512), bf16),
        in_specs=[VM, VM, SM, HBM, HBM],
        out_specs=VM,
        scratch_shapes=[
            pltpu.VMEM((D, 3 * D), bf16), pltpu.VMEM((D, D), bf16), tall, tall,
            pltpu.SemaphoreType.DMA((2, 3)), pltpu.SemaphoreType.DMA,
        ],
        compiler_params=params(52_500_000),
        cost_estimate=cost(5, 10),
        name="spatial",
    )(x, gain_space.reshape(1, D), scale_space, qkv_space, out_space)
    stream = lax.all_to_all(stream.reshape(128, 8, 512), ("tm", "patch"), 0, 0, tiled=True)
    output, chosen = pl.pallas_call(
        temporal_kernel,
        out_shape=[jax.ShapeDtypeStruct((512, D), bf16)] * 2,
        in_specs=[VM, VM, SM, VM, VM, VM, VM],
        out_specs=[HBM, HBM],
        scratch_shapes=[
            pltpu.VMEM((512, D), f32), tall, tall, tall, tall,
            pltpu.SemaphoreType.DMA((2,)), pltpu.SemaphoreType.DMA,
        ],
        compiler_params=params(20_000_000),
        cost_estimate=cost(4, 10),
        name="temporal",
    )(stream, gain_time.reshape(1, D), scale_time, qkv_time, out_time, codes, codebook)
    output = lax.all_to_all(output.reshape(16, 32, D), "tm", 0, 0, tiled=True)
    encoded, commitment = pl.pallas_call(
        final_kernel,
        out_shape=[jax.ShapeDtypeStruct((512, D), bf16)] * 2,
        in_specs=[VM, HBM],
        out_specs=[HBM, HBM],
        scratch_shapes=[pltpu.VMEM((512, D), bf16)] * 3 + [pltpu.SemaphoreType.DMA((9,))],
        input_output_aliases={1: 1},
        compiler_params=params(20_000_000),
        cost_estimate=cost(0.3, 4),
        name="final",
    )(output, chosen)
    return encoded.reshape(8, 64, D), commitment.reshape(8, 64, D)


def solution(mesh):
    rows = P("tm", "patch", None)
    return jax.shard_map(
        shards,
        mesh=mesh,
        in_specs=(rows, P("tm", "patch")) + (P(),) * 9,
        out_specs=(rows, rows),
        check_vma=False,
    )
```

```python
import functools
import math

import jax
import jax.numpy as jnp
from jax import lax
from jax.experimental import pallas as pl
from jax.experimental.pallas import tpu as pltpu
from jax.sharding import PartitionSpec as P

H = 16
HD = 64
D = 1024
GROUP = 256
PAIR = 128
ROWS = 256
LOG2E = math.log2(math.e)
f32 = jnp.float32
bf16 = jnp.bfloat16


def iota(shape, axis):
    return lax.broadcasted_iota(jnp.int32, shape, axis)


def same_head_mean():
    same = (iota((GROUP, GROUP), 0) // HD) == (iota((GROUP, GROUP), 1) // HD)
    return jnp.where(same, f32(1.0 / HD), f32(0.0)).astype(bf16)


def norm_rows(wide, gain):
    mean = jnp.mean(wide * wide, -1, keepdims=True)
    return (wide * lax.rsqrt(mean + 1e-5) * gain).astype(bf16)


def head_norm(block, averager):
    square = (block * block).astype(bf16)
    mean = jnp.dot(square, averager, preferred_element_type=f32)
    return block * lax.rsqrt(mean + 1e-6)


def scale_row(scale_ref, first_head):
    head = iota((1, GROUP), 1) // HD
    row = jnp.full((1, GROUP), scale_ref[first_head], f32)
    for h in range(1, GROUP // HD):
        row = jnp.where(head == h, scale_ref[first_head + h], row)
    return row * f32(LOG2E / HD)


def key_pair(key):
    low = iota(key.shape, 1) < HD
    zero = jnp.zeros_like(key)
    return jnp.concatenate([jnp.where(low, key, zero), jnp.where(low, zero, key)], 0)


def value_pair(value):
    low = iota(value.shape, 1) < HD
    zero = jnp.zeros_like(value)
    one = jnp.ones_like(value)
    first = jnp.concatenate([jnp.where(low, value, zero), jnp.where(low, one, zero)], 1)
    second = jnp.concatenate([jnp.where(low, zero, value), jnp.where(low, zero, one)], 1)
    return jnp.concatenate([first, second], 0)


def project(normed, qkv, scale_ref, averager, g):
    q, k, v = (
        jnp.dot(normed, qkv[:, part * D + g * GROUP : part * D + (g + 1) * GROUP], preferred_element_type=f32)
        for part in range(3)
    )
    q = (head_norm(q, averager) * scale_row(scale_ref, 4 * g)).astype(bf16)
    return q, head_norm(k, averager).astype(bf16), v.astype(bf16)


def weighted_mean(weights, values):
    o = jnp.dot(weights, values, preferred_element_type=f32)
    return (o[:, :PAIR] / o[:, PAIR:]).astype(bf16)


def logits(q, unit):
    lanes, rows, keys, _ = unit
    return lax.dot_general(q[rows, lanes], keys, (((1,), (1,)), ((), ())), preferred_element_type=f32)


def spatial_kernel(
    x, gain, scale_ref, qkv_hbm, out_hbm, o, qkv_buf, out_buf, normed, attn, sems, out_sem
):
    out_copy = pltpu.make_async_copy(out_hbm, out_buf, out_sem)
    copies = [
        [
            pltpu.make_async_copy(
                qkv_hbm.at[:, pl.ds(part * D + start, count)],
                qkv_buf.at[:, pl.ds(part * D + start, count)],
                sems.at[n, part],
            )
            for part in range(3)
        ]
        for n, (start, count) in enumerate(((0, GROUP), (GROUP, D - GROUP)))
    ]
    for copy in copies[0]:
        copy.start()
    for n in range(4):
        rows = slice(128 * n, 128 * (n + 1))
        normed[rows, :] = norm_rows(x[rows, :].astype(f32), gain[...])
    averager = same_head_mean()
    for g in range(4):
        if g < 2:
            for copy in copies[g]:
                copy.wait()
        if g == 0:
            for copy in copies[1] + [out_copy]:
                copy.start()
        q, k, v = project(normed[...], qkv_buf, scale_ref, averager, g)
        units = []
        for pair in range(2):
            lanes = slice(pair * PAIR, (pair + 1) * PAIR)
            keys = key_pair(k[:, lanes])
            values = value_pair(v[:, lanes])
            for r in range(0, 512, ROWS):
                units.append((lanes, slice(r, r + ROWS), keys, values))
        s = logits(q, units[0])
        for n, (lanes, rows, keys, values) in enumerate(units):
            later = logits(q, units[n + 1]) if n + 1 < len(units) else None
            w = jnp.exp2(s).astype(bf16)
            ratio = weighted_mean(w, values)
            attn[rows, g * GROUP + lanes.start : g * GROUP + lanes.stop] = ratio
            s = later
    out_copy.wait()
    half = D // 2
    low = iota((1, 8, half), 1) < 4
    for n in range(2):
        rows = slice(256 * n, 256 * (n + 1))
        stream = x[rows, :].astype(f32) + jnp.dot(attn[rows, :], out_buf[...], preferred_element_type=f32)
        a = stream[:, :half].reshape(32, 8, half)
        b = stream[:, half:].reshape(32, 8, half)
        even = jnp.where(low, a, pltpu.roll(b, 4, 1)).astype(bf16)
        odd = jnp.where(low, pltpu.roll(a, 4, 1), b).astype(bf16)
        for j in range(4):
            runs = jnp.stack([even[8 * j : 8 * j + 8], odd[8 * j : 8 * j + 8]], 1)
            o[:, 4 * n + j] = runs.reshape(16, 8, half)


def temporal_kernel(
    x, gain, scale_ref, qkv_buf, out_buf, codes, codebook, o, chosen_hbm,
    stream, normed, attn, chosen, chosen_sem,
):
    turned = codes[...].astype(f32).T
    for f in range(8):
        hot = jnp.where(turned[:, f : f + 1].astype(jnp.int32) == iota((64, D), 1), f32(1.0), f32(0.0)).astype(bf16)
        o[64 * f : 64 * (f + 1), :] = hot
    half = D // 2
    one = f32(1.0)
    nil = f32(0.0)
    want = iota((128, 256), 0)
    source = (want & 31) * 8 + (want >> 5)
    first = jnp.where(iota((128, 256), 1) == source, one, nil).astype(bf16)
    second = jnp.where(iota((128, 256), 1) == source + 4, one, nil).astype(bf16)
    for b in range(4):
        recv = x[32 * b : 32 * (b + 1)].reshape(256, half)
        block = jnp.concatenate(
            [
                jnp.dot(first, recv, preferred_element_type=f32),
                jnp.dot(second, recv, preferred_element_type=f32),
            ],
            1,
        )
        ready = norm_rows(block, gain[...])
        for p in range(4):
            rows = slice(p * 128 + 32 * b, p * 128 + 32 * (b + 1))
            stream[rows, :] = block[32 * p : 32 * (p + 1)]
            normed[rows, :] = ready[32 * p : 32 * (p + 1)]
    averager = same_head_mean()
    causal = (iota((256, 256), 0) & 127) >= (iota((256, 256), 1) & 127)
    for g in range(4):
        q, k, v = project(normed[...], qkv_buf, scale_ref, averager, g)
        part = slice(g * GROUP, (g + 1) * GROUP)
        chosen[:, part] = jnp.dot(o[...], codebook[:, part], preferred_element_type=f32).astype(bf16)
        for pair in range(2):
            lanes = slice(pair * PAIR, (pair + 1) * PAIR)
            for p in range(0, 4, 2):
                one_rows = slice(p * 128, (p + 1) * 128)
                two_rows = slice((p + 1) * 128, (p + 2) * 128)
                blank = jnp.zeros((128, PAIR), bf16)
                queries = jnp.concatenate(
                    [
                        jnp.concatenate([q[one_rows, lanes], blank], 1),
                        jnp.concatenate([blank, q[two_rows, lanes]], 1),
                    ],
                    0,
                )
                keys = jnp.concatenate([key_pair(k[one_rows, lanes]), key_pair(k[two_rows, lanes])], 1)
                s = lax.dot_general(queries, keys, (((1,), (1,)), ((), ())), preferred_element_type=f32)
                w = jnp.where(causal, jnp.exp2(s), nil).astype(bf16)
                for n, rows in enumerate((one_rows, two_rows)):
                    ratio = weighted_mean(w[n * 128 : (n + 1) * 128], value_pair(v[rows, lanes]))
                    attn[rows, g * GROUP + lanes.start : g * GROUP + lanes.stop] = ratio
    chosen_copy = pltpu.make_async_copy(chosen, chosen_hbm, chosen_sem)
    chosen_copy.start()
    want = iota((256, 256), 0)
    source = (want & 3) * 64 + (want >> 2)
    move = jnp.where(iota((256, 256), 1) == source, one, nil).astype(bf16)
    for b in range(2):
        pick = [slice(p * 128 + 64 * b, p * 128 + 64 * (b + 1)) for p in range(4)]
        mixed = jnp.concatenate([attn[rows, :] for rows in pick], 0)
        base = jnp.concatenate([stream[rows, :] for rows in pick], 0)
        output = (base + jnp.dot(mixed, out_buf[...], preferred_element_type=f32)).astype(bf16)
        rows = pl.ds(256 * b, 256)
        o[rows, :] = jnp.dot(move, output, preferred_element_type=f32).astype(bf16)
    chosen_copy.wait()


def final_kernel(x_ref, chosen_hbm, enc_hbm, com_hbm, chosen, enc, com, sems):
    load = pltpu.make_async_copy(chosen_hbm, chosen, sems.at[0])
    load.start()
    stores = []
    want = iota((128, 128), 0)
    source = ((want >> 2) & 15) * 8 + (want >> 6) * 4 + (want & 3)
    move = jnp.where(iota((128, 128), 1) == source, f32(1.0), f32(0.0)).astype(bf16)
    outputs = []
    for n in range(4):
        rows = pl.ds(n * 128, 128)
        block = x_ref[:, 8 * n : 8 * (n + 1), :].reshape(128, D)
        output = jnp.dot(move, block, preferred_element_type=f32)
        outputs.append(output)
        enc[rows, :] = output.astype(bf16)
        store = pltpu.make_async_copy(enc.at[rows, :], enc_hbm.at[rows, :], sems.at[1 + n])
        store.start()
        stores.append(store)
    load.wait()
    for n, output in enumerate(outputs):
        rows = pl.ds(n * 128, 128)
        com[rows, :] = (output - chosen[rows, :].astype(f32)).astype(bf16)
        store = pltpu.make_async_copy(com.at[rows, :], com_hbm.at[rows, :], sems.at[5 + n])
        store.start()
        stores.append(store)
    for store in stores:
        store.wait()


VM = pl.BlockSpec(memory_space=pltpu.VMEM)
HBM = pl.BlockSpec(memory_space=pltpu.HBM)
SM = pl.BlockSpec(memory_space=pltpu.SMEM)


def params(limit):
    return pltpu.CompilerParams(vmem_limit_bytes=limit)


def cost(gmac, mbytes):
    return pl.CostEstimate(flops=int(2e9 * gmac), bytes_accessed=int(1e6 * mbytes), transcendentals=0)


def shards(frames_in, codes, gain_space, qkv_space, out_space, scale_space, gain_time, qkv_time, out_time, scale_time, codebook):
    x = lax.all_to_all(frames_in, "patch", 0, 0, tiled=True).reshape(512, D)
    tall = pltpu.VMEM((512, D), bf16)
    stream = pl.pallas_call(
        spatial_kernel,
        out_shape=jax.ShapeDtypeStruct((16, 8, 8, 512), bf16),
        in_specs=[VM, VM, SM, HBM, HBM],
        out_specs=VM,
        scratch_shapes=[
            pltpu.VMEM((D, 3 * D), bf16), pltpu.VMEM((D, D), bf16), tall, tall,
            pltpu.SemaphoreType.DMA((2, 3)), pltpu.SemaphoreType.DMA,
        ],
        compiler_params=params(52_500_000),
        cost_estimate=cost(5, 10),
        name="spatial",
    )(x, gain_space.reshape(1, D), scale_space, qkv_space, out_space)
    stream = lax.all_to_all(stream.reshape(128, 8, 512), ("tm", "patch"), 0, 0, tiled=True)
    output, chosen = pl.pallas_call(
        temporal_kernel,
        out_shape=[jax.ShapeDtypeStruct((512, D), bf16)] * 2,
        in_specs=[VM, VM, SM, VM, VM, VM, VM],
        out_specs=[VM, HBM],
        scratch_shapes=[pltpu.VMEM((512, D), f32), tall, tall, tall, pltpu.SemaphoreType.DMA],
        compiler_params=params(20_000_000),
        cost_estimate=cost(4, 10),
        name="temporal",
    )(stream, gain_time.reshape(1, D), scale_time, qkv_time, out_time, codes, codebook)
    output = lax.all_to_all(output.reshape(16, 32, D), "tm", 0, 0, tiled=True)
    encoded, commitment = pl.pallas_call(
        final_kernel,
        out_shape=[jax.ShapeDtypeStruct((512, D), bf16)] * 2,
        in_specs=[VM, HBM],
        out_specs=[HBM, HBM],
        scratch_shapes=[pltpu.VMEM((512, D), bf16)] * 3 + [pltpu.SemaphoreType.DMA((9,))],
        input_output_aliases={1: 1},
        compiler_params=params(20_000_000),
        cost_estimate=cost(0.3, 4),
        name="final",
    )(output, chosen)
    return encoded.reshape(8, 64, D), commitment.reshape(8, 64, D)


def solution(mesh):
    rows = P("tm", "patch", None)
    return jax.shard_map(
        shards,
        mesh=mesh,
        in_specs=(rows, P("tm", "patch")) + (P(),) * 9,
        out_specs=(rows, rows),
        check_vma=False,
    )
```
